32 devices in a mesh: sample: 4 (over z), expert: 8 (over y, x, core).
Axes of the slice: x: 2, y: 2, z: 4, core: 2. Of those that a mesh axis runs over, the one named last changes fastest.
Arguments:
- queries: bfloat16 [64, 4, 8192], P('expert', 'sample'), may hold values from -8 to 8
- prompt_kv: bfloat16 [64, 256, 1024], P('expert', 'sample'), may hold values from -8 to 8
- gen_kv: bfloat16 [64, 4, 32, 1024], P('expert', 'sample'), may hold values from -4 to 4
- gen_lengths: int32 [64, 4], P('expert', 'sample'), may hold values from 1 to 32, 64 in all within a row
- out_proj: bfloat16 [8192, 4096], P(None, 'sample'), may hold values from -1 to 1
- residual: bfloat16 [64, 4, 4096], P('expert', None, 'sample'), may hold values from -160 to 160
- norm_gain: float32 [4096], P('sample'), may hold values from 0.1 to 1.9
- w_gate_up: bfloat16 [24, 4096, 3072], P('expert', 'sample'), may hold values from -0.09375 to 0.09375
- w_down: bfloat16 [24, 1536, 4096], P('expert', None, 'sample'), may hold values from -0.15625 to 0.15625
- routes: int32 [64, 4, 8], P('expert'), may hold values from 0 to 23, all different within a row; in each aligned block of 32 rows (0 to 31, 32 to 63, ..., all dimensions but the last counted through in order) at most 13 rows name the same one
- route_probs: float32 [64, 4, 8], P('expert'), may hold values from 0.1 to 1
Outputs:
- mixed: bfloat16 [64, 4, 4096], P('expert', None, 'sample')
- expert_out: bfloat16 [64, 4, 4096], P('expert', None, 'sample')
The draws below stay inside these ranges and needn't reach their ends.
Inputs may be any that keep to these rules, and one draw needn't show every extreme that they name: `gen_lengths`: in each prompt, at least one sample has 32 generated tokens. `routes`: each row names 8 different experts. Among the 32 rows of the prompts of one index of expert, no expert is named by more than 13 rows, a bound that some block reaches.
All inputs are finite; a program needn't handle non-finite values. No bound on the sum of `gen_lengths` on one device may be relied on, other than what follows from the above.
Results may differ from the reference program's by a relative error of at most 0.028.
Values may be sent and summed in bfloat16 or wider, within the bound.
No kernel may reach another device: no remote copies, remote signals or barrier semaphores. Data moves between devices by JAX's collectives and lax.ppermute only.
A program may use at most 128 MiB of HBM per device.

```python
import math
import jax
import jax.numpy as jnp
import numpy as np
from jax import lax

D = 4096
FF = 1536
QHEADS = 64
KVHEADS = 4
HDIM = 128
TOPK = 8
PROMPTS_DEV = 8
GEN = 32
SAMPLES = 4
PROMPTS = 64
PLEN = 256
WIN_EXPERTS = 24
CAP = 13
N_SAMPLE = 4
N_EXPERT = 8


def draw_queries(key, part):
    shape = (PROMPTS, SAMPLES, QHEADS * HDIM)
    values = jnp.clip(jax.random.normal(jax.random.fold_in(key, 1), shape, jnp.float32), -4.0, 4.0)
    return values.astype(jnp.bfloat16)


def draw_prompt_kv(key, part):
    width = 2 * KVHEADS * HDIM
    shape = (PROMPTS, PLEN, width)
    values = jnp.clip(jax.random.normal(jax.random.fold_in(key, 3), shape, jnp.float32), -4.0, 4.0)
    return values.astype(jnp.bfloat16)


def draw_residual(key, part):
    shape = (PROMPTS, SAMPLES, D)
    feature = jnp.arange(D, dtype=jnp.float32) / D
    values = jnp.clip(jax.random.normal(jax.random.fold_in(key, 5), shape, jnp.float32), -4.0, 4.0)
    row_scale = jnp.exp(jax.random.uniform(jax.random.fold_in(key, 8), (PROMPTS, SAMPLES, 1), jnp.float32, math.log(0.5), math.log(5.0)))
    rising = 1.0 + 2.0 * feature
    return (values * row_scale * rising[None, None, :]).astype(jnp.bfloat16)


def shard_levels(own_key, extent, cuts, least, largest):
    def one(dim, shards_of):
        steps = jax.random.uniform(jax.random.fold_in(jax.random.fold_in(own_key, 6), dim), (shards_of,), jnp.float32, least / len(cuts), largest / len(cuts))
        return jnp.repeat(jnp.exp(steps), extent[dim] // shards_of).reshape((-1,) + (1,) * (len(extent) - dim - 1))

    level = one(*cuts[0])
    for cut in cuts[1:]:
        level = level * one(*cut)
    return level


def length_profile(number_of, total, reach, slope):
    loads = [(1 << 20) // math.isqrt(standing ** slope) + 1 for standing in range(2, number_of + 1)]
    rest, holding = total - reach - (number_of - 1), [1] * (number_of - 1)
    while rest > 0:
        free = [i for i in range(number_of - 1) if holding[i] < reach]
        whole, remaining = sum([loads[i] for i in free]), rest
        for i in free:
            extra = min(reach - holding[i], max(1, remaining * loads[i] // whole), rest)
            holding[i] = holding[i] + extra
            rest = rest - extra
    return np.array([reach] + holding)


def ragged(stream_key, count, total, reach, skew):
    if count == 2:
        one = jax.random.randint(stream_key, (), max(1, total - reach), min(reach, total - 1) + 1)
        return jnp.stack([one, total - one])
    sizes = jnp.asarray(length_profile(count, total, reach, skew), jnp.int32)
    couples = (count - 1) // 2
    donor, sink = sizes[1:1 + 2 * couples:2], sizes[2:2 + 2 * couples:2]
    slack = jnp.minimum(donor - 1, reach - sink)
    shifted = jax.random.randint(jax.random.fold_in(stream_key, 1), (couples,), 0, 1 << 20) % (slack + 1)
    sizes = sizes.at[1:1 + 2 * couples:2].set(donor - shifted).at[2:2 + 2 * couples:2].set(sink + shifted)
    return sizes[jax.random.permutation(jax.random.fold_in(stream_key, 2), count)]


def routed_block(rng, own, number, rows, count, top, most, lean):
    order = jax.random.permutation(rng, count)
    packed, ordinary = portions_of(count, rows * top, most, lean, True), portions_of(count, rows * top, most, lean, False)
    places = jnp.arange(count)

    def named(sizes, offset_by):
        used = int((sizes > 0).sum())
        fixed = max(1, used // 4)
        moved = fixed + (places - fixed + offset_by * (used - fixed)) % max(1, count - fixed)
        return jnp.zeros((count,), jnp.int32).at[order[jnp.where(places < fixed, places, moved)]].set(jnp.asarray(sizes, jnp.int32))

    sizes = jnp.where(number % 4 == 0, named(packed, number // 4), named(ordinary, number - number // 4 - 1))
    mixed = jax.random.permutation(jax.random.fold_in(own, 3), count)
    source_of, sink = mixed[0:count // 2 * 2:2], mixed[1:count // 2 * 2:2]
    margin = jnp.minimum(sizes[source_of] - 1, most - sizes[sink]) // 2
    margin = jnp.where((source_of == order[0]) | (sink == order[0]) | (sizes[sink] == 0), 0, jnp.maximum(margin, 0))
    moved = jax.random.randint(jax.random.fold_in(own, 4), (count // 2,), 0, 1 << 20) % (margin + 1)
    sizes = sizes.at[source_of].add(-moved).at[sink].add(moved)
    labels = jnp.searchsorted(jnp.cumsum(sizes), jnp.arange(rows * top), side="right").astype(jnp.int32)
    table = labels.reshape(top, rows).T
    table = table[jax.random.permutation(jax.random.fold_in(own, 1), rows)]
    offset_by = jax.random.randint(jax.random.fold_in(own, 2), (rows, 1), 0, top)
    return jnp.take_along_axis(table, (jnp.arange(top)[None, :] + offset_by) % top, axis=1)


def portions_of(number_of, total, bound, slope, full):
    portions = [(1 << 20) // math.isqrt(rank ** slope) + 1 for rank in range(1, number_of + 1)]
    largest = bound if full else min(bound, max(-(-total // number_of), total * portions[0] // sum(portions)))
    least = 1 if total - largest >= number_of - 1 else 0
    given, spare = [largest] + [least] * (number_of - 1), total - largest - least * (number_of - 1)
    while spare > 0:
        movable = [i for i in range(1, number_of) if given[i] < largest] or [i for i in range(1, number_of) if given[i] < bound]
        whole, remaining = sum([portions[i] for i in movable]), spare
        for i in movable:
            more = min(bound - given[i], max(1, remaining * portions[i] // whole), spare)
            given[i] = given[i] + more
            spare = spare - more
    return np.array(given)


def centred(stream_key, shape, deviation, most, cuts=(), kind=jnp.bfloat16):
    drawn = jax.random.normal(stream_key, shape, jnp.float32) * deviation
    if len(cuts) > 0:
        drawn = shard_levels(stream_key, shape, cuts, -0.22, 0.18) * drawn
    return jnp.clip(drawn, min=-most, max=most).astype(kind)


def setup_inputs(seed: int = 0) -> dict:
    arg_keys = jax.random.split(jax.random.key(seed), 12)
    queries = draw_queries(jax.random.fold_in(arg_keys[11], 71), 0)
    prompt_kv = draw_prompt_kv(jax.random.fold_in(arg_keys[11], 71), 0)
    gen_kv = centred(arg_keys[2], (PROMPTS, SAMPLES, GEN, 2 * KVHEADS * HDIM), 1.0, 4.0, ((0, 8), (1, 4)))
    gen_lengths = jax.vmap(lambda own: ragged(own, SAMPLES, SAMPLES * GEN // 2, GEN, 2))(jax.random.split(arg_keys[3], PROMPTS)).reshape((PROMPTS, SAMPLES)).astype(jnp.int32)
    out_proj = centred(arg_keys[4], (QHEADS * HDIM, D), (max(QHEADS * HDIM // 256, 1)) ** -0.5, 1.0, ((1, 4),))
    residual = draw_residual(jax.random.fold_in(arg_keys[11], 71), 0)
    norm_gain = jnp.clip(1.0 + 0.18 * jax.random.normal(arg_keys[6], (D,), jnp.float32), 0.1, 1.9)
    w_gate_up = centred(arg_keys[7], (WIN_EXPERTS, D, 2 * FF), D ** -0.5, 0.09375, ((0, 8), (1, 4)))
    w_down = centred(arg_keys[8], (WIN_EXPERTS, FF, D), FF ** -0.5, 0.15625, ((0, 8), (2, 4)))
    routes_keys = jax.random.split(jax.random.fold_in(arg_keys[9], 1), PROMPTS * SAMPLES // (PROMPTS_DEV * SAMPLES))
    routes_turns = jax.random.permutation(jax.random.fold_in(arg_keys[9], 3), PROMPTS * SAMPLES // (PROMPTS_DEV * SAMPLES))
    routes = jax.vmap(lambda own, number: routed_block(jax.random.fold_in(arg_keys[9], 2), own, number, PROMPTS_DEV * SAMPLES, WIN_EXPERTS, TOPK, CAP, 2))(routes_keys, routes_turns).reshape((PROMPTS, SAMPLES, TOPK))
    route_probs = jnp.clip(jnp.exp(math.log(1.0) - 2.3025851 * jax.random.uniform(arg_keys[10], (PROMPTS, SAMPLES, TOPK), jnp.float32) ** shard_levels(arg_keys[10], (PROMPTS, SAMPLES, TOPK), ((0, 8),), -0.2, 0.2)), 0.1, 1.0)
    return {"queries": queries, "prompt_kv": prompt_kv, "gen_kv": gen_kv, "gen_lengths": gen_lengths, "out_proj": out_proj, "residual": residual, "norm_gain": norm_gain, "w_gate_up": w_gate_up, "w_down": w_down, "routes": routes, "route_probs": route_probs}


NEGATIVE = -1e+30
EPSILON = 1e-06

def attend_prompt(operands):
    query, prompt, cache, lengths = operands
    kv_width = KVHEADS * HDIM
    groups = QHEADS // KVHEADS
    scale = HDIM ** (-0.5)
    heads = query.astype(jnp.float32).reshape(SAMPLES, KVHEADS, groups, HDIM)
    prompt_keys = prompt[:, :kv_width].astype(jnp.float32).reshape(PLEN, KVHEADS, HDIM)
    prompt_values = prompt[:, kv_width:].astype(jnp.float32).reshape(PLEN, KVHEADS, HDIM)
    cache_keys = cache[:, :, :kv_width].astype(jnp.float32).reshape(SAMPLES, GEN, KVHEADS, HDIM)
    cache_values = cache[:, :, kv_width:].astype(jnp.float32).reshape(SAMPLES, GEN, KVHEADS, HDIM)
    prompt_scores = jnp.einsum('shgd,nhd->shgn', heads, prompt_keys, precision=lax.Precision.HIGHEST) * scale
    cache_scores = jnp.einsum('shgd,sthd->shgt', heads, cache_keys, precision=lax.Precision.HIGHEST) * scale
    valid = jnp.arange(GEN, dtype=jnp.int32)[None, :] < lengths[:, None]
    cache_scores = jnp.where(valid[:, None, None, :], cache_scores, NEGATIVE)
    highest = jnp.maximum(lax.optimization_barrier(jnp.max(prompt_scores, axis=-1)), lax.optimization_barrier(jnp.max(cache_scores, axis=-1)))
    prompt_weights = jnp.exp(prompt_scores - highest[..., None])
    cache_weights = jnp.exp(cache_scores - highest[..., None])
    weight_sum = lax.optimization_barrier(jnp.sum(prompt_weights, axis=-1)) + lax.optimization_barrier(jnp.sum(cache_weights, axis=-1))
    numerator = jnp.einsum('shgn,nhd->shgd', prompt_weights, prompt_values, precision=lax.Precision.HIGHEST)
    numerator = numerator + jnp.einsum('shgt,sthd->shgd', cache_weights, cache_values, precision=lax.Precision.HIGHEST)
    return (numerator / weight_sum[..., None]).reshape(SAMPLES, QHEADS * HDIM).astype(jnp.bfloat16)

def reference(queries, prompt_kv, gen_kv, gen_lengths, out_proj, residual, norm_gain, w_gate_up, w_down, routes, route_probs):
    attended = lax.map(attend_prompt, (queries, prompt_kv, gen_kv, gen_lengths))
    projected = jnp.dot(attended.reshape(-1, QHEADS * HDIM), out_proj, preferred_element_type=jnp.float32)
    projected = projected.reshape(PROMPTS, SAMPLES, D)
    mixed = projected.astype(jnp.bfloat16)
    stream = residual.astype(jnp.float32) + projected
    factor = lax.rsqrt(lax.optimization_barrier(jnp.sum(stream * stream, axis=-1)) / D + EPSILON)
    normed = (stream * factor[..., None] * norm_gain).astype(jnp.bfloat16).reshape(-1, D)
    expert_ids = routes.reshape(-1, TOPK)
    route_weight = route_probs.reshape(-1, TOPK)
    block_width = D // N_SAMPLE
    limit = N_EXPERT * CAP

    def one_expert(running, expert):
        chosen = expert_ids == expert
        weight = lax.optimization_barrier(jnp.sum(jnp.where(chosen, route_weight, 0.0), axis=1))
        flagged = jnp.any(chosen, axis=1).astype(jnp.int32)
        order = jnp.argsort(1 - flagged, stable=True)[:limit].astype(jnp.int32)
        picked = normed[order].astype(jnp.float32).reshape(limit, N_SAMPLE, block_width)
        blocks = w_gate_up[expert].astype(jnp.float32).reshape(N_SAMPLE, block_width, 2 * FF)
        partial_sums = jnp.einsum('nbd,bdf->nbf', picked, blocks, precision=lax.Precision.HIGHEST)
        rounded = lax.optimization_barrier(partial_sums.astype(jnp.bfloat16))
        gate_up = lax.optimization_barrier(jnp.sum(rounded.astype(jnp.float32), axis=1))
        activated = (jax.nn.silu(gate_up[:, :FF]) * gate_up[:, FF:]).astype(jnp.bfloat16)
        finished = jnp.dot(activated, w_down[expert], preferred_element_type=jnp.float32).astype(jnp.bfloat16)
        finished = lax.optimization_barrier(finished).astype(jnp.float32)
        return (running.at[order].add(finished * weight[order][:, None]), None)
    running = jnp.zeros((normed.shape[0], D), jnp.float32)
    running, unused = lax.scan(one_expert, running, jnp.arange(WIN_EXPERTS, dtype=jnp.int32))
    expert_out = running.astype(jnp.bfloat16).reshape(PROMPTS, SAMPLES, D)
    return (mixed, expert_out)
```

```python
import functools

import jax
import jax.numpy as jnp
from jax import lax
from jax.experimental import pallas as pl
from jax.experimental.pallas import tpu as pltpu
from jax.sharding import PartitionSpec as P

KVHEADS = 4
HDIM = 128
TOPK = 8
NEGATIVE = -1e30
EPSILON = 1e-06
MIB = 1 << 20


def send(array, axis, size, shift):
    return lax.ppermute(array, axis, [(i, (i + shift) % size) for i in range(size)])


def swap(array, axis, size, bits):
    return lax.ppermute(array, axis, [(i, i ^ bits) for i in range(size)])


def block_scores(keys, query, tokens, groups, bound):
    scores = lax.dot_general(
        keys, query, (((1,), (1,)), ((), ())), preferred_element_type=jnp.float32
    ) * (HDIM**-0.5)
    row = lax.broadcasted_iota(jnp.int32, scores.shape, 0)
    lane = lax.broadcasted_iota(jnp.int32, scores.shape, 1)
    keep = row // tokens == (lane // groups) % KVHEADS
    if bound is not None:
        keep = keep & (row % tokens < bound)
    return jnp.where(keep, scores, NEGATIVE)


def stacked_heads(rows, first):
    return jnp.concatenate(
        [rows[:, (first + h) * HDIM : (first + h + 1) * HDIM] for h in range(KVHEADS)], axis=0
    )


def softmax_part(scores, values):
    highest = jnp.max(scores, axis=0, keepdims=True)
    weights = jnp.exp(scores - highest)
    total = jnp.sum(weights, axis=0, keepdims=True)
    numerator = lax.dot_general(
        weights.astype(jnp.bfloat16),
        values,
        (((0,), (0,)), ((), ())),
        preferred_element_type=jnp.float32,
    )
    return highest, total, numerator


def prompt_kernel(samples, *refs):
    query_refs, cache_ref = refs[:samples], refs[samples]
    out_refs, stat_ref = refs[samples + 1 : 2 * samples + 1], refs[2 * samples + 1]
    prompts, tokens, _ = cache_ref.shape
    heads = query_refs[0].shape[1]
    for p in range(prompts):
        rows = cache_ref[p]
        keys, values = stacked_heads(rows, 0), stacked_heads(rows, KVHEADS)
        for pair in range(samples // 2):
            query = jnp.concatenate([query_refs[2 * pair][p], query_refs[2 * pair + 1][p]], axis=0)
            scores = block_scores(keys, query, tokens, heads // KVHEADS, None)
            highest, total, numerator = softmax_part(scores, values)
            out_refs[2 * pair][p] = numerator[:heads].astype(jnp.bfloat16)
            out_refs[2 * pair + 1][p] = numerator[heads:].astype(jnp.bfloat16)
            stat_ref[pair, 0, p : p + 1, :] = highest
            stat_ref[pair, 1, p : p + 1, :] = total


def gen_kernel(length_ref, query_ref, cache_ref, out_ref, stat_ref):
    prompts, tokens, _ = cache_ref.shape
    heads = query_ref.shape[1]
    for p in range(prompts):
        rows = cache_ref[p]
        keys, values = stacked_heads(rows, 0), stacked_heads(rows, KVHEADS)
        scores = block_scores(keys, query_ref[p], tokens, heads // KVHEADS, length_ref[p])
        highest, total, numerator = softmax_part(scores, values)
        out_ref[p] = numerator
        stat_ref[0, p : p + 1, :] = highest
        stat_ref[1, p : p + 1, :] = total


VMEM_SPEC = pl.BlockSpec(memory_space=pltpu.VMEM)
SMEM_SPEC = pl.BlockSpec(memory_space=pltpu.SMEM)


def prompt_part(queries, cache):
    samples = len(queries)
    shape = queries[0].shape
    results = pl.pallas_call(
        functools.partial(prompt_kernel, samples),
        out_shape=[jax.ShapeDtypeStruct(shape, jnp.bfloat16)] * samples
        + [jax.ShapeDtypeStruct((samples // 2, 2, shape[0], 2 * shape[1]), jnp.float32)],
        in_specs=[VMEM_SPEC] * (samples + 1),
        out_specs=[VMEM_SPEC] * (samples + 1),
        compiler_params=pltpu.CompilerParams(vmem_limit_bytes=32 * MIB),
        cost_estimate=pl.CostEstimate(
            flops=1000 * 1000 * 1000, bytes_accessed=4 * MIB, transcendentals=500 * 1000
        ),
    )(*queries, cache)
    stats = results[samples]
    heads = shape[1]
    return results[:samples], [
        stats[k // 2, :, :, (k % 2) * heads : (k % 2 + 1) * heads] for k in range(samples)
    ]


def gen_part(query, cache, lengths):
    shape = query.shape
    return pl.pallas_call(
        gen_kernel,
        out_shape=[
            jax.ShapeDtypeStruct(shape, jnp.float32),
            jax.ShapeDtypeStruct((2, shape[0], shape[1]), jnp.float32),
        ],
        in_specs=[SMEM_SPEC, VMEM_SPEC, VMEM_SPEC],
        out_specs=[VMEM_SPEC, VMEM_SPEC],
        compiler_params=pltpu.CompilerParams(vmem_limit_bytes=32 * MIB),
        cost_estimate=pl.CostEstimate(
            flops=100 * 1000 * 1000, bytes_accessed=2 * MIB, transcendentals=100 * 1000
        ),
    )(lengths, query, cache)


def project_kernel(samples, features, place_ref, *refs):
    attended_refs = refs[:samples]
    weight_ref, residual_ref, gain_ref, mixed_ref, row_ref, total_ref, order_ref = refs[samples:]
    step = pl.program_id(0)
    prompts = attended_refs[0].shape[0]

    @pl.when(step == 0)
    def _():
        total_ref[...] = jnp.zeros_like(total_ref)

    stacked = jnp.concatenate([r[...] for r in attended_refs], axis=0)
    total_ref[...] += jnp.dot(stacked, weight_ref[...], preferred_element_type=jnp.float32)

    @pl.when(step == pl.num_programs(0) - 1)
    def _():
        for k in range(samples):
            s = lax.rem(place_ref[0] - k + samples, samples)
            order_ref[pl.ds(pl.multiple_of(s * prompts, prompts), prompts), :] = total_ref[
                k * prompts : (k + 1) * prompts, :
            ]
        projected = order_ref[...]
        mixed_ref[...] = projected.astype(jnp.bfloat16)
        stream = residual_ref[...].astype(jnp.float32) + projected
        square = jnp.sum(stream * stream, axis=1, keepdims=True)
        high = square.astype(jnp.bfloat16).astype(jnp.float32)
        low = square - high
        row_ref[:, :features] = (stream * gain_ref[...]).astype(jnp.bfloat16)
        lane = lax.broadcasted_iota(jnp.int32, (square.shape[0], HDIM), 1)
        row_ref[:, features:] = jnp.where(
            lane == 0, high, jnp.where(lane == 1, low, 0.0)
        ).astype(jnp.bfloat16)


def project(attended, out_proj, residual, gain, place):
    samples = len(attended)
    prompts, inner = attended[0].shape
    width = out_proj.shape[1]
    rows = samples * prompts
    depth = 1024
    whole = lambda shape: pl.BlockSpec(shape, lambda i, place: (0, 0))
    return pl.pallas_call(
        functools.partial(project_kernel, samples, width),
        out_shape=[
            jax.ShapeDtypeStruct((rows, width), jnp.bfloat16),
            jax.ShapeDtypeStruct((rows, width + HDIM), jnp.bfloat16),
        ],
        grid_spec=pltpu.PrefetchScalarGridSpec(
            num_scalar_prefetch=1,
            grid=(inner // depth,),
            in_specs=[pl.BlockSpec((prompts, depth), lambda i, place: (0, i))] * samples
            + [
                pl.BlockSpec((depth, width), lambda i, place: (i, 0)),
                whole((rows, width)),
                whole((1, width)),
            ],
            out_specs=[whole((rows, width)), whole((rows, width + HDIM))],
            scratch_shapes=[
                pltpu.VMEM((rows, width), jnp.float32),
                pltpu.VMEM((rows, width), jnp.float32),
            ],
        ),
        compiler_params=pltpu.CompilerParams(vmem_limit_bytes=32 * MIB),
        cost_estimate=pl.CostEstimate(
            flops=2 * rows * inner * width, bytes_accessed=2 * inner * width, transcendentals=0
        ),
    )(place, *attended, out_proj, residual, gain)


def gate_kernel(features, place_ref, pick_ref, near_ref, far_ref, gate_ref, up_ref, *rest):
    out_refs, chosen_ref = rest[:-1], rest[-1]
    step = pl.program_id(0)
    half = near_ref.shape[0]

    @pl.when(step == 0)
    def _():
        pick = pick_ref[...]
        chosen = jnp.dot(
            pick[:, :half], near_ref[:, :features], preferred_element_type=jnp.float32
        ) + jnp.dot(pick[:, half:], far_ref[:, :features], preferred_element_type=jnp.float32)
        chosen_ref[...] = chosen.astype(jnp.bfloat16)

    chosen = chosen_ref[...]
    part = gate_ref.shape[1]
    gate = jnp.dot(chosen, gate_ref[...], preferred_element_type=jnp.float32)
    up = jnp.dot(chosen, up_ref[...], preferred_element_type=jnp.float32)
    for k, out_ref in enumerate(out_refs):

        @pl.when(step == (k - 1) % len(out_refs))
        def _():
            out_ref[:, :part] = gate.astype(jnp.bfloat16)
            out_ref[:, part:] = up.astype(jnp.bfloat16)


def gate_up_parts(pick, near, far, weights, expert, place, samples):
    slots, rows = pick.shape
    _, features, wide = weights.shape
    hidden = wide // 2
    part = hidden // samples
    if part % HDIM:
        chosen = jnp.dot(
            pick,
            jnp.concatenate([near, far], axis=0)[:, :features],
            preferred_element_type=jnp.float32,
        ).astype(jnp.bfloat16)
        shares = jnp.dot(chosen, weights[expert], preferred_element_type=jnp.float32)
        shares = shares.astype(jnp.bfloat16).reshape(slots, 2, samples, part)
        shares = jnp.roll(shares, -place[0], axis=2)
        return [shares[:, :, k].reshape(slots, 2 * part) for k in range(samples)]
    whole = lambda shape: pl.BlockSpec(shape, lambda i, place: (0, 0))
    column = lambda i, place: lax.rem(place[0] + i + 1, samples)
    return pl.pallas_call(
        functools.partial(gate_kernel, features),
        out_shape=[jax.ShapeDtypeStruct((slots, 2 * part), jnp.bfloat16)] * samples,
        grid_spec=pltpu.PrefetchScalarGridSpec(
            num_scalar_prefetch=1,
            grid=(samples,),
            in_specs=[
                whole(pick.shape),
                whole(near.shape),
                whole(far.shape),
                pl.BlockSpec(
                    (None, features, part), lambda i, place: (expert, 0, column(i, place))
                ),
                pl.BlockSpec(
                    (None, features, part), lambda i, place: (expert, 0, samples + column(i, place))
                ),
            ],
            out_specs=[whole((slots, 2 * part))] * samples,
            scratch_shapes=[pltpu.VMEM((slots, features), jnp.bfloat16)],
        ),
        compiler_params=pltpu.CompilerParams(vmem_limit_bytes=32 * MIB),
        cost_estimate=pl.CostEstimate(
            flops=2 * slots * features * wide, bytes_accessed=2 * features * wide, transcendentals=0
        ),
    )(place, pick, near, far, weights, weights)


def down_kernel(place_ref, *refs):
    samples = len(refs) - 3
    act_refs, (weight_ref, out_ref, total_ref) = refs[:samples], refs[samples:]
    step = pl.program_id(0)
    for k, act_ref in enumerate(act_refs):

        @pl.when(step == k)
        def _():
            share = jnp.dot(act_ref[...], weight_ref[...], preferred_element_type=jnp.float32)
            if k == 0:
                total_ref[...] = share
            elif k < samples - 1:
                total_ref[...] += share
            else:
                out_ref[...] = (total_ref[...] + share).astype(jnp.bfloat16)


def down_rows(acts, weights, expert, place):
    samples = len(acts)
    slots, part = acts[0].shape
    _, hidden, width = weights.shape
    if part % HDIM:
        joined = jnp.stack(acts, axis=1)[:, ::-1]
        joined = jnp.roll(joined, place[0] + 1, axis=1).reshape(slots, hidden)
        return jnp.dot(joined, weights[expert], preferred_element_type=jnp.float32).astype(
            jnp.bfloat16
        )
    whole = lambda shape: pl.BlockSpec(shape, lambda i, place: (0, 0))
    return pl.pallas_call(
        down_kernel,
        out_shape=jax.ShapeDtypeStruct((slots, width), jnp.bfloat16),
        grid_spec=pltpu.PrefetchScalarGridSpec(
            num_scalar_prefetch=1,
            grid=(samples,),
            in_specs=[whole((slots, part))] * samples
            + [
                pl.BlockSpec(
                    (None, part, width),
                    lambda i, place: (expert, lax.rem(place[0] - i + samples, samples), 0),
                )
            ],
            out_specs=whole((slots, width)),
            scratch_shapes=[pltpu.VMEM((slots, width), jnp.float32)],
        ),
        compiler_params=pltpu.CompilerParams(vmem_limit_bytes=32 * MIB),
        cost_estimate=pl.CostEstimate(
            flops=2 * slots * hidden * width, bytes_accessed=2 * hidden * width, transcendentals=0
        ),
    )(place, *acts, weights)


def gather_experts(array, owners):
    near = jnp.concatenate(
        [array] + [swap(array, "expert", owners, b) for b in range(2, owners, 2)], axis=0
    )
    return near, swap(near, "expert", owners, 1)


def on_device(
    queries,
    prompt_kv,
    gen_kv,
    gen_lengths,
    out_proj,
    residual,
    norm_gain,
    w_gate_up,
    w_down,
    routes,
    route_probs,
):
    samples, owners = lax.axis_size("sample"), lax.axis_size("expert")
    place = lax.axis_index("sample").astype(jnp.int32).reshape(1)
    prompts = queries.shape[0]
    heads = queries.shape[2] // HDIM
    width = residual.shape[2]
    rows = prompts * samples
    per_owner = w_gate_up.shape[0]
    hidden = w_down.shape[1]
    part = hidden // samples

    query = queries.reshape(prompts, heads, HDIM)
    all_queries = [query] + [send(query, "sample", samples, k) for k in range(1, samples)]

    by_sample = lambda a: jnp.swapaxes(a, 0, 1).reshape(rows, TOPK)
    table = jnp.concatenate(
        [by_sample(routes).astype(jnp.float32), by_sample(route_probs)], axis=1
    )
    table = jnp.concatenate(gather_experts(table, owners), axis=0)
    capacity = 5 * rows * TOPK // (4 * per_owner * owners)
    slots = owners * capacity
    first = lax.axis_index("expert") * per_owner
    mine = (first + jnp.arange(per_owner, dtype=jnp.int32)).astype(jnp.float32)
    match = table[None, :, :TOPK] == mine[:, None, None]
    hit = jnp.any(match, axis=2)
    weight = jnp.sum(jnp.where(match, table[None, :, TOPK:], 0.0), axis=2)
    hit_blocks = hit.reshape(per_owner, owners, rows)
    earlier = (jnp.arange(rows)[:, None] < jnp.arange(rows)[None, :]).astype(jnp.bfloat16)
    rank = jnp.einsum(
        "jbr,rq->jbq",
        hit_blocks.astype(jnp.bfloat16),
        earlier,
        preferred_element_type=jnp.float32,
    ).astype(jnp.int32)
    slot = rank + capacity * jnp.arange(owners, dtype=jnp.int32)[None, :, None]
    slot = jnp.where(hit_blocks, slot, -1).reshape(per_owner, owners * rows)
    chosen = slot[:, None, :] == jnp.arange(slots, dtype=jnp.int32)[None, :, None]
    pick = chosen.astype(jnp.bfloat16)
    slot_weight = jnp.sum(jnp.where(chosen, weight[:, None, :], 0.0), axis=2)

    gen_out, gen_stat = gen_part(query, gen_kv[:, 0], gen_lengths[:, 0])
    parts, stats = prompt_part(all_queries, prompt_kv)
    outs, marks = [gen_out, parts[0]], [gen_stat, stats[0]]
    for k in range(1, samples):
        outs.append(send(parts[k], "sample", samples, -k))
        marks.append(send(stats[k], "sample", samples, -k))
    highest = functools.reduce(jnp.maximum, [m[0] for m in marks])
    scales = [jnp.exp(m[0] - highest) for m in marks]
    total = sum(c * m[1] for c, m in zip(scales, marks))
    attended = sum(
        o.astype(jnp.float32) * (c / total)[:, :, None] for o, c in zip(outs, scales)
    )
    attended = attended.astype(jnp.bfloat16).reshape(prompts, heads * HDIM)
    attended = [attended] + [send(attended, "sample", samples, k) for k in range(1, samples)]
    mixed, row_block = project(
        attended,
        out_proj,
        jnp.swapaxes(residual, 0, 1).reshape(rows, width),
        norm_gain.reshape(1, width),
        place,
    )
    mixed = jnp.swapaxes(mixed.reshape(samples, prompts, width), 0, 1)

    near, far = gather_experts(row_block, owners)
    square = jnp.concatenate([near[:, width : width + 2], far[:, width : width + 2]], axis=0)
    square = jnp.sum(square.astype(jnp.float32), axis=1)
    square = square + sum(send(square, "sample", samples, k) for k in range(1, samples))
    factor = lax.rsqrt(square / (width * samples) + EPSILON)
    slot_factor = jnp.sum(jnp.where(chosen, factor[None, None, :], 0.0), axis=2)

    finished = []
    for j in range(per_owner):
        shares = gate_up_parts(pick[j], near, far, w_gate_up, j, place, samples)
        gate_up = shares[0].astype(jnp.float32)
        for k in range(1, samples):
            gate_up = gate_up + send(shares[k], "sample", samples, k).astype(jnp.float32)
        gate_up = gate_up * slot_factor[j][:, None]
        act = jax.nn.silu(gate_up[:, :part]) * gate_up[:, part:] * slot_weight[j][:, None]
        act = act.astype(jnp.bfloat16)
        acts = [act] + [send(act, "sample", samples, k) for k in range(1, samples)]
        finished.append(down_rows(acts, w_down, j, place))
    returned = sum(
        lax.dot_general(
            pick[j], finished[j], (((0,), (0,)), ((), ())), preferred_element_type=jnp.float32
        )
        for j in range(per_owner)
    )
    returned = returned.reshape(2, owners // 2, rows, width)
    arrived = swap(returned[1].astype(jnp.bfloat16), "expert", owners, 1)
    paired = returned[0] + arrived.astype(jnp.float32)
    outgoing = paired.astype(jnp.bfloat16)
    combined = paired[0]
    for b in range(1, owners // 2):
        combined = combined + swap(outgoing[b], "expert", owners, 2 * b).astype(jnp.float32)
    expert_out = combined.astype(jnp.bfloat16).reshape(samples, prompts, width)
    return mixed, jnp.swapaxes(expert_out, 0, 1)


def solution(mesh):
    placed = (
        P("expert", "sample", None),
        P("expert", "sample", None),
        P("expert", "sample", None, None),
        P("expert", "sample"),
        P(None, "sample"),
        P("expert", None, "sample"),
        P("sample"),
        P("expert", "sample", None),
        P("expert", None, "sample"),
        P("expert", None, None),
        P("expert", None, None),
    )
    return jax.shard_map(
        on_device,
        mesh=mesh,
        in_specs=placed,
        out_specs=(P("expert", None, "sample"), P("expert", None, "sample")),
        check_vma=False,
    )
```

```python
import functools

import jax
import jax.numpy as jnp
from jax import lax
from jax.experimental import pallas as pl
from jax.experimental.pallas import tpu as pltpu
from jax.sharding import PartitionSpec as P

KVHEADS = 4
HDIM = 128
TOPK = 8
NEGATIVE = -1e30
EPSILON = 1e-06
MIB = 1 << 20
SCOPED = 10 * MIB


def send(array, axis, size, shift):
    return lax.ppermute(array, axis, [(i, (i + shift) % size) for i in range(size)])


def swap(array, axis, size, bits):
    return lax.ppermute(array, axis, [(i, i ^ bits) for i in range(size)])


def block_scores(keys, query, tokens, groups, bound):
    scores = lax.dot_general(
        keys, query, (((1,), (1,)), ((), ())), preferred_element_type=jnp.float32
    ) * (HDIM**-0.5)
    row = lax.broadcasted_iota(jnp.int32, scores.shape, 0)
    lane = lax.broadcasted_iota(jnp.int32, scores.shape, 1)
    keep = row // tokens == (lane // groups) % KVHEADS
    if bound is not None:
        keep = keep & (row % tokens < bound)
    return jnp.where(keep, scores, NEGATIVE)


def stacked_heads(rows, first):
    return jnp.concatenate(
        [rows[:, (first + h) * HDIM : (first + h + 1) * HDIM] for h in range(KVHEADS)], axis=0
    )


def softmax_part(scores, values):
    highest = jnp.max(scores, axis=0, keepdims=True)
    weights = jnp.exp(scores - highest)
    total = jnp.sum(weights, axis=0, keepdims=True)
    numerator = lax.dot_general(
        weights.astype(jnp.bfloat16),
        values,
        (((0,), (0,)), ((), ())),
        preferred_element_type=jnp.float32,
    )
    return highest, total, numerator


def prompt_kernel(samples, *refs):
    query_refs, cache_ref = refs[:samples], refs[samples]
    out_refs, stat_ref = refs[samples + 1 : 2 * samples + 1], refs[2 * samples + 1]
    prompts, tokens, _ = cache_ref.shape
    heads = query_refs[0].shape[1]
    for p in range(prompts):
        rows = cache_ref[p]
        keys, values = stacked_heads(rows, 0), stacked_heads(rows, KVHEADS)
        for pair in range(samples // 2):
            query = jnp.concatenate([query_refs[2 * pair][p], query_refs[2 * pair + 1][p]], axis=0)
            scores = block_scores(keys, query, tokens, heads // KVHEADS, None)
            highest, total, numerator = softmax_part(scores, values)
            out_refs[2 * pair][p] = numerator[:heads].astype(jnp.bfloat16)
            out_refs[2 * pair + 1][p] = numerator[heads:].astype(jnp.bfloat16)
            stat_ref[pair, 0, p : p + 1, :] = highest
            stat_ref[pair, 1, p : p + 1, :] = total


def gen_kernel(length_ref, query_ref, cache_ref, out_ref, stat_ref):
    prompts, tokens, _ = cache_ref.shape
    heads = query_ref.shape[1]
    for p in range(prompts):
        rows = cache_ref[p]
        keys, values = stacked_heads(rows, 0), stacked_heads(rows, KVHEADS)
        scores = block_scores(keys, query_ref[p], tokens, heads // KVHEADS, length_ref[p])
        highest, total, numerator = softmax_part(scores, values)
        out_ref[p] = numerator
        stat_ref[0, p : p + 1, :] = highest
        stat_ref[1, p : p + 1, :] = total


VMEM_SPEC = pl.BlockSpec(memory_space=pltpu.VMEM)
ANY_SPEC = pl.BlockSpec(memory_space=pl.ANY)
SMEM_SPEC = pl.BlockSpec(memory_space=pltpu.SMEM)


def in_hbm(array):
    return pltpu.with_memory_space_constraint(array, pltpu.HBM)


def prompt_part(queries, cache):
    samples = len(queries)
    shape = queries[0].shape
    results = pl.pallas_call(
        functools.partial(prompt_kernel, samples),
        out_shape=[jax.ShapeDtypeStruct(shape, jnp.bfloat16)] * samples
        + [jax.ShapeDtypeStruct((samples // 2, 2, shape[0], 2 * shape[1]), jnp.float32)],
        in_specs=[VMEM_SPEC] * (samples + 1),
        out_specs=[VMEM_SPEC] * (samples + 1),
        compiler_params=pltpu.CompilerParams(vmem_limit_bytes=SCOPED),
        cost_estimate=pl.CostEstimate(
            flops=1000 * 1000 * 1000, bytes_accessed=4 * MIB, transcendentals=500 * 1000
        ),
    )(*queries, cache)
    stats = results[samples]
    heads = shape[1]
    return results[:samples], [
        stats[k // 2, :, :, (k % 2) * heads : (k % 2 + 1) * heads] for k in range(samples)
    ]


def gen_part(query, cache, lengths):
    shape = query.shape
    return pl.pallas_call(
        gen_kernel,
        out_shape=[
            jax.ShapeDtypeStruct(shape, jnp.float32),
            jax.ShapeDtypeStruct((2, shape[0], shape[1]), jnp.float32),
        ],
        in_specs=[SMEM_SPEC, VMEM_SPEC, VMEM_SPEC],
        out_specs=[VMEM_SPEC, VMEM_SPEC],
        compiler_params=pltpu.CompilerParams(vmem_limit_bytes=SCOPED),
        cost_estimate=pl.CostEstimate(
            flops=100 * 1000 * 1000, bytes_accessed=2 * MIB, transcendentals=100 * 1000
        ),
    )(lengths, query, cache)


def project_kernel(samples, features, place_ref, *refs):
    attended_refs = refs[:samples]
    weight_ref, residual_ref, gain_ref, mixed_ref, row_ref, order_ref, held_ref, sems = refs[samples:]
    prompts = attended_refs[0].shape[0]
    pieces = sems.shape[0]
    depth = weight_ref.shape[0] // pieces
    copies = []
    for i in range(pieces):
        piece = pl.ds(i * depth, depth)
        copies.append(pltpu.make_async_copy(weight_ref.at[piece], held_ref.at[piece], sems.at[i]))
        copies[i].start()
    stacked = jnp.concatenate([r[...] for r in attended_refs], axis=0)
    total = jnp.zeros(order_ref.shape, jnp.float32)
    for i in range(pieces):
        copies[i].wait()
        total = total + jnp.dot(
            stacked[:, i * depth : (i + 1) * depth],
            held_ref[i * depth : (i + 1) * depth, :],
            preferred_element_type=jnp.float32,
        )
    for k in range(samples):
        s = lax.rem(place_ref[0] - k + samples, samples)
        order_ref[pl.ds(pl.multiple_of(s * prompts, prompts), prompts), :] = total[
            k * prompts : (k + 1) * prompts, :
        ]
    projected = order_ref[...]
    mixed_ref[...] = projected.astype(jnp.bfloat16)
    stream = residual_ref[...].astype(jnp.float32) + projected
    square = jnp.sum(stream * stream, axis=1, keepdims=True)
    high = square.astype(jnp.bfloat16).astype(jnp.float32)
    low = square - high
    row_ref[:, :features] = (stream * gain_ref[...]).astype(jnp.bfloat16)
    lane = lax.broadcasted_iota(jnp.int32, (square.shape[0], HDIM), 1)
    row_ref[:, features:] = jnp.where(lane == 0, high, jnp.where(lane == 1, low, 0.0)).astype(
        jnp.bfloat16
    )


def project(attended, out_proj, residual, gain, place):
    samples = len(attended)
    prompts, inner = attended[0].shape
    width = out_proj.shape[1]
    rows = samples * prompts
    return pl.pallas_call(
        functools.partial(project_kernel, samples, width),
        out_shape=[
            jax.ShapeDtypeStruct((rows, width), jnp.bfloat16),
            jax.ShapeDtypeStruct((rows, width + HDIM), jnp.bfloat16),
        ],
        in_specs=[SMEM_SPEC] + [VMEM_SPEC] * samples + [ANY_SPEC] + [VMEM_SPEC] * 2,
        out_specs=[VMEM_SPEC] * 2,
        scratch_shapes=[
            pltpu.VMEM((rows, width), jnp.float32),
            pltpu.VMEM(out_proj.shape, jnp.bfloat16),
            pltpu.SemaphoreType.DMA((8,)),
        ],
        compiler_params=pltpu.CompilerParams(vmem_limit_bytes=SCOPED + 2 * inner * width),
        cost_estimate=pl.CostEstimate(
            flops=2 * rows * inner * width, bytes_accessed=2 * inner * width, transcendentals=0
        ),
    )(place, *attended, in_hbm(out_proj), residual, gain)


def gate_kernel(features, expert, place_ref, pick_ref, near_ref, far_ref, weight_ref, *refs):
    out_refs, held_ref, sems = refs[:-2], refs[-2], refs[-1]
    half = near_ref.shape[0]
    samples = len(out_refs)
    hidden = weight_ref.shape[2] // 2
    part = hidden // samples
    order = list(range(1, samples)) + [0]
    copies = {}
    for k in order:
        column = lax.rem(place_ref[0] + k, samples) * part
        for side in range(2):
            columns = pl.ds(pl.multiple_of(side * hidden + column, HDIM), part)
            copies[k, side] = pltpu.make_async_copy(
                weight_ref.at[expert, :, columns], held_ref.at[k, side], sems.at[k, side]
            )
            copies[k, side].start()
    pick = pick_ref[...]
    chosen = jnp.dot(
        pick[:, :half], near_ref[:, :features], preferred_element_type=jnp.float32
    ) + jnp.dot(pick[:, half:], far_ref[:, :features], preferred_element_type=jnp.float32)
    chosen = chosen.astype(jnp.bfloat16)
    for k in order:
        for side in range(2):
            copies[k, side].wait()
            out_refs[k][:, side * part : (side + 1) * part] = jnp.dot(
                chosen, held_ref[k, side], preferred_element_type=jnp.float32
            ).astype(jnp.bfloat16)


def gate_up_parts(pick, near, far, weights, expert, place, samples):
    slots, rows = pick.shape
    _, features, wide = weights.shape
    hidden = wide // 2
    part = hidden // samples
    if part % HDIM:
        chosen = jnp.dot(
            pick,
            jnp.concatenate([near, far], axis=0)[:, :features],
            preferred_element_type=jnp.float32,
        ).astype(jnp.bfloat16)
        shares = jnp.dot(chosen, weights[expert], preferred_element_type=jnp.float32)
        shares = shares.astype(jnp.bfloat16).reshape(slots, 2, samples, part)
        shares = jnp.roll(shares, -place[0], axis=2)
        return [shares[:, :, k].reshape(slots, 2 * part) for k in range(samples)]
    return pl.pallas_call(
        functools.partial(gate_kernel, features, expert),
        out_shape=[jax.ShapeDtypeStruct((slots, 2 * part), jnp.bfloat16)] * samples,
        in_specs=[SMEM_SPEC] + [VMEM_SPEC] * 3 + [ANY_SPEC],
        out_specs=[VMEM_SPEC] * samples,
        scratch_shapes=[
            pltpu.VMEM((samples, 2, features, part), jnp.bfloat16),
            pltpu.SemaphoreType.DMA((samples, 2)),
        ],
        compiler_params=pltpu.CompilerParams(vmem_limit_bytes=SCOPED + 2 * features * wide),
        cost_estimate=pl.CostEstimate(
            flops=2 * slots * features * wide, bytes_accessed=2 * features * wide, transcendentals=0
        ),
    )(place, pick, near, far, in_hbm(weights))


def down_kernel(expert, place_ref, *refs):
    samples = len(refs) - 2
    act_refs, (weight_ref, out_ref) = refs[:samples], refs[samples:]
    part = act_refs[0].shape[1]
    total = None
    for k, act_ref in enumerate(act_refs):
        row = lax.rem(place_ref[0] - k + samples, samples) * part
        share = jnp.dot(
            act_ref[...],
            weight_ref[expert, pl.ds(pl.multiple_of(row, HDIM), part), :],
            preferred_element_type=jnp.float32,
        )
        total = share if total is None else total + share
    out_ref[...] = total.astype(jnp.bfloat16)


def down_rows(acts, weights, expert, place):
    samples = len(acts)
    slots, part = acts[0].shape
    _, hidden, width = weights.shape
    if part % HDIM:
        joined = jnp.stack(acts, axis=1)[:, ::-1]
        joined = jnp.roll(joined, place[0] + 1, axis=1).reshape(slots, hidden)
        return jnp.dot(joined, weights[expert], preferred_element_type=jnp.float32).astype(
            jnp.bfloat16
        )
    return pl.pallas_call(
        functools.partial(down_kernel, expert),
        out_shape=jax.ShapeDtypeStruct((slots, width), jnp.bfloat16),
        in_specs=[SMEM_SPEC] + [VMEM_SPEC] * (samples + 1),
        out_specs=VMEM_SPEC,
        compiler_params=pltpu.CompilerParams(vmem_limit_bytes=SCOPED),
        cost_estimate=pl.CostEstimate(
            flops=2 * slots * hidden * width, bytes_accessed=2 * hidden * width, transcendentals=0
        ),
    )(place, *acts, weights)


def gather_experts(array, owners):
    near = jnp.concatenate(
        [array] + [swap(array, "expert", owners, b) for b in range(2, owners, 2)], axis=0
    )
    return near, swap(near, "expert", owners, 1)


def on_device(
    queries,
    prompt_kv,
    gen_kv,
    gen_lengths,
    out_proj,
    residual,
    norm_gain,
    w_gate_up,
    w_down,
    routes,
    route_probs,
):
    samples, owners = lax.axis_size("sample"), lax.axis_size("expert")
    place = lax.axis_index("sample").astype(jnp.int32).reshape(1)
    prompts = queries.shape[0]
    heads = queries.shape[2] // HDIM
    width = residual.shape[2]
    rows = prompts * samples
    per_owner = w_gate_up.shape[0]
    hidden = w_down.shape[1]
    part = hidden // samples

    query = queries.reshape(prompts, heads, HDIM)
    all_queries = [query] + [send(query, "sample", samples, k) for k in range(1, samples)]

    by_sample = lambda a: jnp.swapaxes(a, 0, 1).reshape(rows, TOPK)
    table = jnp.concatenate(
        [by_sample(routes).astype(jnp.float32), by_sample(route_probs)], axis=1
    )
    table = jnp.concatenate(gather_experts(table, owners), axis=0)
    capacity = 5 * rows * TOPK // (4 * per_owner * owners)
    slots = owners * capacity
    first = lax.axis_index("expert") * per_owner
    mine = (first + jnp.arange(per_owner, dtype=jnp.int32)).astype(jnp.float32)
    match = table[None, :, :TOPK] == mine[:, None, None]
    hit = jnp.any(match, axis=2)
    weight = jnp.sum(jnp.where(match, table[None, :, TOPK:], 0.0), axis=2)
    hit_blocks = hit.reshape(per_owner, owners, rows)
    earlier = (jnp.arange(rows)[:, None] < jnp.arange(rows)[None, :]).astype(jnp.bfloat16)
    rank = jnp.einsum(
        "jbr,rq->jbq",
        hit_blocks.astype(jnp.bfloat16),
        earlier,
        preferred_element_type=jnp.float32,
    ).astype(jnp.int32)
    slot = rank + capacity * jnp.arange(owners, dtype=jnp.int32)[None, :, None]
    slot = jnp.where(hit_blocks, slot, -1).reshape(per_owner, owners * rows)
    chosen = slot[:, None, :] == jnp.arange(slots, dtype=jnp.int32)[None, :, None]
    pick = chosen.astype(jnp.bfloat16)
    slot_weight = jnp.sum(jnp.where(chosen, weight[:, None, :], 0.0), axis=2)

    gen_out, gen_stat = gen_part(query, gen_kv[:, 0], gen_lengths[:, 0])
    parts, stats = prompt_part(all_queries, prompt_kv)
    outs, marks = [gen_out, parts[0]], [gen_stat, stats[0]]
    for k in range(1, samples):
        outs.append(send(parts[k], "sample", samples, -k))
        marks.append(send(stats[k], "sample", samples, -k))
    highest = functools.reduce(jnp.maximum, [m[0] for m in marks])
    scales = [jnp.exp(m[0] - highest) for m in marks]
    total = sum(c * m[1] for c, m in zip(scales, marks))
    attended = sum(
        o.astype(jnp.float32) * (c / total)[:, :, None] for o, c in zip(outs, scales)
    )
    attended = attended.astype(jnp.bfloat16).reshape(prompts, heads * HDIM)
    attended = [attended] + [send(attended, "sample", samples, k) for k in range(1, samples)]
    mixed, row_block = project(
        attended,
        out_proj,
        jnp.swapaxes(residual, 0, 1).reshape(rows, width),
        norm_gain.reshape(1, width),
        place,
    )
    mixed = jnp.swapaxes(mixed.reshape(samples, prompts, width), 0, 1)

    near, far = gather_experts(row_block, owners)
    square = jnp.concatenate([near[:, width : width + 2], far[:, width : width + 2]], axis=0)
    square = jnp.sum(square.astype(jnp.float32), axis=1)
    square = square + sum(send(square, "sample", samples, k) for k in range(1, samples))
    factor = lax.rsqrt(square / (width * samples) + EPSILON)
    slot_factor = jnp.sum(jnp.where(chosen, factor[None, None, :], 0.0), axis=2)

    finished = []
    for j in range(per_owner):
        shares = gate_up_parts(pick[j], near, far, w_gate_up, j, place, samples)
        gate_up = shares[0].astype(jnp.float32)
        for k in range(1, samples):
            gate_up = gate_up + send(shares[k], "sample", samples, k).astype(jnp.float32)
        gate_up = gate_up * slot_factor[j][:, None]
        act = jax.nn.silu(gate_up[:, :part]) * gate_up[:, part:] * slot_weight[j][:, None]
        act = act.astype(jnp.bfloat16)
        acts = [act] + [send(act, "sample", samples, k) for k in range(1, samples)]
        finished.append(down_rows(acts, w_down, j, place))
    returned = sum(
        lax.dot_general(
            pick[j], finished[j], (((0,), (0,)), ((), ())), preferred_element_type=jnp.float32
        )
        for j in range(per_owner)
    )
    returned = returned.reshape(2, owners // 2, rows, width)
    arrived = swap(returned[1].astype(jnp.bfloat16), "expert", owners, 1)
    paired = returned[0] + arrived.astype(jnp.float32)
    outgoing = paired.astype(jnp.bfloat16)
    combined = paired[0]
    for b in range(1, owners // 2):
        combined = combined + swap(outgoing[b], "expert", owners, 2 * b).astype(jnp.float32)
    expert_out = combined.astype(jnp.bfloat16).reshape(samples, prompts, width)
    return mixed, jnp.swapaxes(expert_out, 0, 1)


def solution(mesh):
    placed = (
        P("expert", "sample", None),
        P("expert", "sample", None),
        P("expert", "sample", None, None),
        P("expert", "sample"),
        P(None, "sample"),
        P("expert", None, "sample"),
        P("sample"),
        P("expert", "sample", None),
        P("expert", None, "sample"),
        P("expert", None, None),
        P("expert", None, None),
    )
    return jax.shard_map(
        on_device,
        mesh=mesh,
        in_specs=placed,
        out_specs=(P("expert", None, "sample"), P("expert", None, "sample")),
        check_vma=False,
    )
```

```python
import functools

import jax
import jax.numpy as jnp
from jax import lax
from jax.experimental import pallas as pl
from jax.experimental.pallas import tpu as pltpu
from jax.sharding import PartitionSpec as P

KVHEADS = 4
HDIM = 128
TOPK = 8
NEGATIVE = -1e30
EPSILON = 1e-06
DIRECT = ()
MIB = 1 << 20
SCOPED = 10 * MIB


def send(array, axis, size, shift):
    return lax.ppermute(array, axis, [(i, (i + shift) % size) for i in range(size)])


def swap(array, axis, size, bits):
    return lax.ppermute(array, axis, [(i, i ^ bits) for i in range(size)])


def block_scores(keys, query, tokens, groups, bound):
    scores = lax.dot_general(
        keys, query, (((1,), (1,)), ((), ())), preferred_element_type=jnp.float32
    ) * (HDIM**-0.5)
    row = lax.broadcasted_iota(jnp.int32, scores.shape, 0)
    lane = lax.broadcasted_iota(jnp.int32, scores.shape, 1)
    keep = row // tokens == (lane // groups) % KVHEADS
    if bound is not None:
        keep = keep & (row % tokens < bound)
    return jnp.where(keep, scores, NEGATIVE)


def stacked_heads(rows, first):
    return jnp.concatenate(
        [rows[:, (first + h) * HDIM : (first + h + 1) * HDIM] for h in range(KVHEADS)], axis=0
    )


def softmax_part(scores, values):
    highest = jnp.max(scores, axis=0, keepdims=True)
    weights = jnp.exp(scores - highest)
    total = jnp.sum(weights, axis=0, keepdims=True)
    numerator = lax.dot_general(
        weights.astype(jnp.bfloat16),
        values,
        (((0,), (0,)), ((), ())),
        preferred_element_type=jnp.float32,
    )
    return highest, total, numerator


def prompt_kernel(samples, *refs):
    query_refs, cache_ref, out_refs = refs[:samples], refs[samples], refs[samples + 1 :]
    prompts, tokens, _ = cache_ref.shape
    heads = query_refs[0].shape[1]
    marks = [[] for _ in range(samples // 2)]
    for p in range(prompts):
        rows = cache_ref[p]
        keys, values = stacked_heads(rows, 0), stacked_heads(rows, KVHEADS)
        for pair in range(samples // 2):
            query = jnp.concatenate([query_refs[2 * pair][p], query_refs[2 * pair + 1][p]], axis=0)
            scores = block_scores(keys, query, tokens, heads // KVHEADS, None)
            highest, total, numerator = softmax_part(scores, values)
            out_refs[2 * pair][p] = numerator[:heads].astype(jnp.bfloat16)
            out_refs[2 * pair + 1][p] = numerator[heads:].astype(jnp.bfloat16)
            marks[pair].append((highest, total))
    for pair, found in enumerate(marks):
        highest = jnp.concatenate([m[0] for m in found], axis=0)
        total = jnp.concatenate([m[1] for m in found], axis=0)
        rows = in_parts(highest, 3) + in_parts(total, 2)
        spare = out_refs[0].shape[0] * heads - prompts * (heads + len(rows))
        rows = rows + [jnp.zeros((spare, rows[0].shape[1]), jnp.float32)]
        slab = jnp.concatenate(rows, axis=0).astype(jnp.bfloat16)
        for i in range(slab.shape[0] // heads):
            for k in (2 * pair, 2 * pair + 1):
                out_refs[k][prompts + i] = slab[i * heads : (i + 1) * heads]


def in_parts(values, count):
    parts = []
    for _ in range(count):
        parts.append(values.astype(jnp.bfloat16).astype(jnp.float32))
        values = values - parts[-1]
    return parts


def gen_kernel(length_ref, query_ref, cache_ref, out_ref, stat_ref):
    prompts, tokens, _ = cache_ref.shape
    heads = query_ref.shape[1]
    for p in range(prompts):
        rows = cache_ref[p]
        keys, values = stacked_heads(rows, 0), stacked_heads(rows, KVHEADS)
        scores = block_scores(keys, query_ref[p], tokens, heads // KVHEADS, length_ref[p])
        highest, total, numerator = softmax_part(scores, values)
        out_ref[p] = numerator
        stat_ref[0, p : p + 1, :] = highest
        stat_ref[1, p : p + 1, :] = total


VMEM_SPEC = pl.BlockSpec(memory_space=pltpu.VMEM)
ANY_SPEC = pl.BlockSpec(memory_space=pl.ANY)
SMEM_SPEC = pl.BlockSpec(memory_space=pltpu.SMEM)


def in_hbm(array):
    return pltpu.with_memory_space_constraint(array, pltpu.HBM)


def prompt_part(queries, cache):
    samples = len(queries)
    prompts, heads, _ = queries[0].shape
    slabs = -(-5 * prompts // heads)
    return pl.pallas_call(
        functools.partial(prompt_kernel, samples),
        out_shape=[jax.ShapeDtypeStruct((prompts + slabs, heads, HDIM), jnp.bfloat16)] * samples,
        in_specs=[VMEM_SPEC] * (samples + 1),
        out_specs=[VMEM_SPEC] * samples,
        compiler_params=pltpu.CompilerParams(vmem_limit_bytes=SCOPED),
        cost_estimate=pl.CostEstimate(
            flops=1000 * 1000 * 1000, bytes_accessed=4 * MIB, transcendentals=500 * 1000
        ),
    )(*queries, cache)


def part_marks(part, prompts, k):
    heads = part.shape[1]
    slab = part[prompts:].reshape(-1, HDIM)[:, k % 2 * heads : (k % 2 + 1) * heads]
    slab = slab.astype(jnp.float32)
    rows = [slab[i * prompts : (i + 1) * prompts] for i in range(5)]
    return rows[0] + rows[1] + rows[2], rows[3] + rows[4]


def gen_part(query, cache, lengths):
    shape = query.shape
    return pl.pallas_call(
        gen_kernel,
        out_shape=[
            jax.ShapeDtypeStruct(shape, jnp.float32),
            jax.ShapeDtypeStruct((2, shape[0], shape[1]), jnp.float32),
        ],
        in_specs=[SMEM_SPEC, VMEM_SPEC, VMEM_SPEC],
        out_specs=[VMEM_SPEC, VMEM_SPEC],
        compiler_params=pltpu.CompilerParams(vmem_limit_bytes=SCOPED),
        cost_estimate=pl.CostEstimate(
            flops=100 * 1000 * 1000, bytes_accessed=2 * MIB, transcendentals=100 * 1000
        ),
    )(lengths, query, cache)


def project_kernel(samples, features, place_ref, *refs):
    attended_refs = refs[:samples]
    weight_ref, residual_ref, gain_ref, mixed_ref, row_ref, order_ref, held_ref, sems = refs[samples:]
    prompts = attended_refs[0].shape[0]
    pieces = sems.shape[0]
    depth = weight_ref.shape[0] // pieces
    copies = []
    for i in range(pieces):
        piece = pl.ds(i * depth, depth)
        copies.append(pltpu.make_async_copy(weight_ref.at[piece], held_ref.at[piece], sems.at[i]))
        copies[i].start()
    stacked = jnp.concatenate([r[...] for r in attended_refs], axis=0)
    total = jnp.zeros(order_ref.shape, jnp.float32)
    for i in range(pieces):
        copies[i].wait()
        total = total + jnp.dot(
            stacked[:, i * depth : (i + 1) * depth],
            held_ref[i * depth : (i + 1) * depth, :],
            preferred_element_type=jnp.float32,
        )
    for k in range(samples):
        s = lax.rem(place_ref[0] - k + samples, samples)
        order_ref[pl.ds(pl.multiple_of(s * prompts, prompts), prompts), :] = total[
            k * prompts : (k + 1) * prompts, :
        ]
    projected = order_ref[...]
    mixed_ref[...] = projected.astype(jnp.bfloat16)
    stream = residual_ref[...].astype(jnp.float32) + projected
    square = jnp.sum(stream * stream, axis=1, keepdims=True)
    high = square.astype(jnp.bfloat16).astype(jnp.float32)
    low = square - high
    row_ref[:, :features] = (stream * gain_ref[...]).astype(jnp.bfloat16)
    lane = lax.broadcasted_iota(jnp.int32, (square.shape[0], HDIM), 1)
    row_ref[:, features:] = jnp.where(lane == 0, high, jnp.where(lane == 1, low, 0.0)).astype(
        jnp.bfloat16
    )


def project(attended, out_proj, residual, gain, place):
    samples = len(attended)
    prompts, inner = attended[0].shape
    width = out_proj.shape[1]
    rows = samples * prompts
    return pl.pallas_call(
        functools.partial(project_kernel, samples, width),
        out_shape=[
            jax.ShapeDtypeStruct((rows, width), jnp.bfloat16),
            jax.ShapeDtypeStruct((rows, width + HDIM), jnp.bfloat16),
        ],
        in_specs=[SMEM_SPEC] + [VMEM_SPEC] * samples + [ANY_SPEC] + [VMEM_SPEC] * 2,
        out_specs=[VMEM_SPEC] * 2,
        scratch_shapes=[
            pltpu.VMEM((rows, width), jnp.float32),
            pltpu.VMEM(out_proj.shape, jnp.bfloat16),
            pltpu.SemaphoreType.DMA((8,)),
        ],
        compiler_params=pltpu.CompilerParams(vmem_limit_bytes=SCOPED + 2 * inner * width),
        cost_estimate=pl.CostEstimate(
            flops=2 * rows * inner * width, bytes_accessed=2 * inner * width, transcendentals=0
        ),
    )(place, *attended, in_hbm(out_proj), residual, gain)


def gate_kernel(features, expert, place_ref, pick_ref, near_ref, far_ref, weight_ref, *refs):
    keep_refs, give_ref, held_ref, sems = refs[:-3], refs[-3], refs[-2], refs[-1]
    half = near_ref.shape[0]
    samples = 2 * len(keep_refs)
    hidden = weight_ref.shape[2] // 2
    part = hidden // samples
    order = list(range(1, samples, 2)) + list(range(samples - 2, -1, -2))
    copies = {}
    for m in order:
        column = lax.bitwise_xor(place_ref[0], m) * part
        for side in range(2):
            columns = pl.ds(pl.multiple_of(side * hidden + column, HDIM), part)
            copies[m, side] = pltpu.make_async_copy(
                weight_ref.at[expert, :, columns], held_ref.at[m, side], sems.at[m, side]
            )
            copies[m, side].start()
    pick = pick_ref[...]
    chosen = jnp.dot(
        pick[:, :half], near_ref[:, :features], preferred_element_type=jnp.float32
    ) + jnp.dot(pick[:, half:], far_ref[:, :features], preferred_element_type=jnp.float32)
    chosen = chosen.astype(jnp.bfloat16)
    for m in order:
        out_ref = give_ref.at[m // 2] if m % 2 else keep_refs[m // 2]
        for side in range(2):
            copies[m, side].wait()
            out_ref[:, side * part : (side + 1) * part] = jnp.dot(
                chosen, held_ref[m, side], preferred_element_type=jnp.float32
            ).astype(jnp.bfloat16)


def gate_up_parts(pick, near, far, weights, expert, place, samples):
    slots, rows = pick.shape
    _, features, wide = weights.shape
    hidden = wide // 2
    part = hidden // samples
    if part % HDIM:
        chosen = jnp.dot(
            pick,
            jnp.concatenate([near, far], axis=0)[:, :features],
            preferred_element_type=jnp.float32,
        ).astype(jnp.bfloat16)
        shares = jnp.dot(chosen, weights[expert], preferred_element_type=jnp.float32)
        shares = shares.astype(jnp.bfloat16).reshape(slots, 2, samples, part)
        wanted = (jnp.bitwise_xor(place[0], jnp.arange(samples))[:, None] == jnp.arange(samples)).astype(
            jnp.bfloat16
        )
        shares = jnp.einsum("mn,sgnp->msgp", wanted, shares, preferred_element_type=jnp.float32)
        shares = shares.astype(jnp.bfloat16).reshape(samples, slots, 2 * part)
        return [shares[m] for m in range(0, samples, 2)], shares[1::2]
    one = jax.ShapeDtypeStruct((slots, 2 * part), jnp.bfloat16)
    results = pl.pallas_call(
        functools.partial(gate_kernel, features, expert),
        out_shape=[one] * (samples // 2)
        + [jax.ShapeDtypeStruct((samples // 2, slots, 2 * part), jnp.bfloat16)],
        in_specs=[SMEM_SPEC] + [VMEM_SPEC] * 3 + [ANY_SPEC],
        out_specs=[VMEM_SPEC] * (samples // 2 + 1),
        scratch_shapes=[
            pltpu.VMEM((samples, 2, features, part), jnp.bfloat16),
            pltpu.SemaphoreType.DMA((samples, 2)),
        ],
        compiler_params=pltpu.CompilerParams(vmem_limit_bytes=SCOPED + 2 * features * wide),
        cost_estimate=pl.CostEstimate(
            flops=2 * slots * features * wide, bytes_accessed=2 * features * wide, transcendentals=0
        ),
    )(place, pick, near, far, in_hbm(weights))
    return results[:-1], results[-1]


def first_swap(keep, give, samples, direct):
    if not direct:
        return swap(give, "sample", samples, 1)
    shares = [give[m // 2] if m % 2 else keep[m // 2] for m in range(samples)]
    return [swap(shares[m], "sample", samples, m) for m in range(1, samples)]


def reduce_parts(keep, give, arrived, samples, direct):
    if direct:
        return sum((a.astype(jnp.float32) for a in arrived), keep[0].astype(jnp.float32))
    bits = 1
    while True:
        keep = [a.astype(jnp.float32) + arrived[i].astype(jnp.float32) for i, a in enumerate(keep)]
        bits *= 2
        if bits == samples:
            return keep[0]
        arrived = swap(
            jnp.stack([a.astype(jnp.bfloat16) for a in keep[1::2]]), "sample", samples, bits
        )
        keep = keep[0::2]


def gather_parts(act, samples, direct):
    if direct:
        acts = [act] + [swap(act, "sample", samples, m) for m in range(1, samples)]
        return jnp.stack(acts[0::2]), jnp.stack(acts[1::2]), list(range(0, samples, 2))
    held, order, bits = [act], [0], samples // 2
    while bits > 1:
        arrived = swap(jnp.stack(held), "sample", samples, bits)
        held = held + [arrived[i] for i in range(len(held))]
        order = order + [m + bits for m in order]
        bits //= 2
    near = jnp.stack(held)
    return near, swap(near, "sample", samples, 1), order


def down_kernel(expert, order, place_ref, near_ref, far_ref, weight_ref, out_ref, held_ref, sems):
    part = near_ref.shape[2]
    known = [(m + odd, i, act_ref) for i, m in enumerate(order) for odd, act_ref in enumerate((near_ref, far_ref))]
    copies = []
    for n, (m, _, _) in enumerate(known):
        row = pl.multiple_of(lax.bitwise_xor(place_ref[0], m) * part, HDIM)
        copies.append(
            pltpu.make_async_copy(
                weight_ref.at[expert, pl.ds(row, part)], held_ref.at[n], sems.at[n]
            )
        )
        copies[n].start()
    total = None
    for n, (_, i, act_ref) in enumerate(known):
        copies[n].wait()
        share = jnp.dot(act_ref[i], held_ref[n], preferred_element_type=jnp.float32)
        total = share if total is None else total + share
    out_ref[...] = total.astype(jnp.bfloat16)


def down_rows(near, far, order, weights, expert, place):
    pairs, slots, part = near.shape
    _, hidden, width = weights.shape
    if part % HDIM:
        known = jnp.array(order + [m + 1 for m in order], jnp.int32)
        held = jnp.bitwise_xor(place[0], known)[None, :] == jnp.arange(2 * pairs)[:, None]
        joined = jnp.einsum(
            "ni,isp->snp",
            held.astype(jnp.bfloat16),
            jnp.concatenate([near, far], axis=0),
            preferred_element_type=jnp.float32,
        )
        joined = joined.astype(jnp.bfloat16).reshape(slots, hidden)
        return jnp.dot(joined, weights[expert], preferred_element_type=jnp.float32).astype(
            jnp.bfloat16
        )
    return pl.pallas_call(
        functools.partial(down_kernel, expert, order),
        out_shape=jax.ShapeDtypeStruct((slots, width), jnp.bfloat16),
        in_specs=[SMEM_SPEC] + [VMEM_SPEC] * 2 + [ANY_SPEC],
        out_specs=VMEM_SPEC,
        scratch_shapes=[
            pltpu.VMEM((2 * pairs, part, width), jnp.bfloat16),
            pltpu.SemaphoreType.DMA((2 * pairs,)),
        ],
        compiler_params=pltpu.CompilerParams(vmem_limit_bytes=SCOPED + 2 * hidden * width),
        cost_estimate=pl.CostEstimate(
            flops=2 * slots * hidden * width, bytes_accessed=2 * hidden * width, transcendentals=0
        ),
    )(place, near, far, in_hbm(weights))


def gather_experts(array, owners):
    near = jnp.concatenate(
        [array] + [swap(array, "expert", owners, b) for b in range(2, owners, 2)], axis=0
    )
    return near, swap(near, "expert", owners, 1)


def on_device(
    queries,
    prompt_kv,
    gen_kv,
    gen_lengths,
    out_proj,
    residual,
    norm_gain,
    w_gate_up,
    w_down,
    routes,
    route_probs,
):
    samples, owners = lax.axis_size("sample"), lax.axis_size("expert")
    place = lax.axis_index("sample").astype(jnp.int32).reshape(1)
    prompts = queries.shape[0]
    heads = queries.shape[2] // HDIM
    width = residual.shape[2]
    rows = prompts * samples
    per_owner = w_gate_up.shape[0]
    hidden = w_down.shape[1]
    part = hidden // samples

    query = queries.reshape(prompts, heads, HDIM)
    all_queries = [query] + [send(query, "sample", samples, k) for k in range(1, samples)]

    gen_out, gen_stat = gen_part(query, gen_kv[:, 0], gen_lengths[:, 0])
    parts = list(prompt_part(all_queries, prompt_kv))
    parts = [parts[0]] + [send(parts[k], "sample", samples, -k) for k in range(1, samples)]
    outs = [gen_out] + [part[:prompts] for part in parts]
    marks = [(gen_stat[0], gen_stat[1])] + [
        part_marks(part, prompts, k) for k, part in enumerate(parts)
    ]
    highest = functools.reduce(jnp.maximum, [m[0] for m in marks])
    scales = [jnp.exp(m[0] - highest) for m in marks]
    total = sum(c * m[1] for c, m in zip(scales, marks))
    attended = sum(
        o.astype(jnp.float32) * (c / total)[:, :, None] for o, c in zip(outs, scales)
    )
    attended = attended.astype(jnp.bfloat16).reshape(prompts, heads * HDIM)
    attended = [attended] + [send(attended, "sample", samples, k) for k in range(1, samples)]
    routes, route_probs, attended[1] = lax.optimization_barrier((routes, route_probs, attended[1]))
    mixed, row_block = project(
        attended,
        out_proj,
        jnp.swapaxes(residual, 0, 1).reshape(rows, width),
        norm_gain.reshape(1, width),
        place,
    )
    mixed = jnp.swapaxes(mixed.reshape(samples, prompts, width), 0, 1)

    by_sample = lambda a: jnp.swapaxes(a, 0, 1).reshape(rows, TOPK)
    table = jnp.concatenate(
        [by_sample(routes).astype(jnp.float32), by_sample(route_probs)], axis=1
    )
    table = jnp.concatenate(gather_experts(table, owners), axis=0)
    capacity = 5 * rows * TOPK // (4 * per_owner * owners)
    slots = owners * capacity
    first = lax.axis_index("expert") * per_owner
    mine = (first + jnp.arange(per_owner, dtype=jnp.int32)).astype(jnp.float32)
    match = table[None, :, :TOPK] == mine[:, None, None]
    hit = jnp.any(match, axis=2)
    weight = jnp.sum(jnp.where(match, table[None, :, TOPK:], 0.0), axis=2)
    hit_blocks = hit.reshape(per_owner, owners, rows)
    earlier = (jnp.arange(rows)[:, None] < jnp.arange(rows)[None, :]).astype(jnp.bfloat16)
    rank = jnp.einsum(
        "jbr,rq->jbq",
        hit_blocks.astype(jnp.bfloat16),
        earlier,
        preferred_element_type=jnp.float32,
    ).astype(jnp.int32)
    slot = rank + capacity * jnp.arange(owners, dtype=jnp.int32)[None, :, None]
    slot = jnp.where(hit_blocks, slot, -1).reshape(per_owner, owners * rows)
    chosen = slot[:, None, :] == jnp.arange(slots, dtype=jnp.int32)[None, :, None]
    pick = chosen.astype(jnp.bfloat16)
    slot_weight = jnp.sum(jnp.where(chosen, weight[:, None, :], 0.0), axis=2)

    near, far = gather_experts(row_block, owners)
    finished = []
    shares, first_hop = [], []
    for j in range(per_owner):
        keep, give = gate_up_parts(pick[j], near, far, w_gate_up, j, place, samples)
        arrived = first_swap(keep, give, samples, j in DIRECT)
        if 0 < j < per_owner - 1:
            near, far, shares[j - 1] = lax.optimization_barrier((near, far, shares[j - 1]))
        shares.append((keep, give, arrived))
    near, far, shares[-1] = lax.optimization_barrier((near, far, shares[-1]))
    square = jnp.concatenate([near[:, width : width + 2], far[:, width : width + 2]], axis=0)
    square = jnp.sum(square.astype(jnp.float32), axis=1)
    square = square + sum(send(square, "sample", samples, k) for k in range(1, samples))
    factor = lax.rsqrt(square / (width * samples) + EPSILON)
    slot_factor = jnp.sum(jnp.where(chosen, factor[None, None, :], 0.0), axis=2)

    for j in range(per_owner):
        gate_up = reduce_parts(*shares[j], samples, j in DIRECT)
        gate_up = gate_up * slot_factor[j][:, None]
        act = jax.nn.silu(gate_up[:, :part]) * gate_up[:, part:] * slot_weight[j][:, None]
        act = act.astype(jnp.bfloat16)
        finished.append(down_rows(*gather_parts(act, samples, j in DIRECT), w_down, j, place))
    returned = sum(
        lax.dot_general(
            pick[j], finished[j], (((0,), (0,)), ((), ())), preferred_element_type=jnp.float32
        )
        for j in range(per_owner)
    )
    returned = returned.reshape(2, owners // 2, rows, width)
    arrived = swap(returned[1].astype(jnp.bfloat16), "expert", owners, 1)
    paired = returned[0] + arrived.astype(jnp.float32)
    outgoing = paired.astype(jnp.bfloat16)
    combined = paired[0]
    for b in range(1, owners // 2):
        combined = combined + swap(outgoing[b], "expert", owners, 2 * b).astype(jnp.float32)
    expert_out = combined.astype(jnp.bfloat16).reshape(samples, prompts, width)
    return mixed, jnp.swapaxes(expert_out, 0, 1)


def solution(mesh):
    placed = (
        P("expert", "sample", None),
        P("expert", "sample", None),
        P("expert", "sample", None, None),
        P("expert", "sample"),
        P(None, "sample"),
        P("expert", None, "sample"),
        P("sample"),
        P("expert", "sample", None),
        P("expert", None, "sample"),
        P("expert", None, None),
        P("expert", None, None),
    )
    return jax.shard_map(
        on_device,
        mesh=mesh,
        in_specs=placed,
        out_specs=(P("expert", None, "sample"), P("expert", None, "sample")),
        check_vma=False,
    )
```

```python
import functools
import math

import jax
import jax.numpy as jnp
from jax import lax
from jax.experimental import pallas as pl
from jax.experimental.pallas import tpu as pltpu
from jax.sharding import PartitionSpec as P

KVHEADS = 4
HDIM = 128
TOPK = 8
NEGATIVE = -1e30
EPSILON = 1e-06
MIB = 1 << 20
SCOPED = 10 * MIB


def send(array, axis, size, shift):
    return lax.ppermute(array, axis, [(i, (i + shift) % size) for i in range(size)])


def swap(array, axis, size, bits):
    return lax.ppermute(array, axis, [(i, i ^ bits) for i in range(size)])


def block_scores(keys, query, tokens, groups, bound):
    scores = lax.dot_general(
        keys, query, (((1,), (1,)), ((), ())), preferred_element_type=jnp.float32
    ) * (HDIM**-0.5)
    row = lax.broadcasted_iota(jnp.int32, scores.shape, 0)
    lane = lax.broadcasted_iota(jnp.int32, scores.shape, 1)
    keep = row // tokens == (lane // groups) % KVHEADS
    if bound is not None:
        keep = keep & (row % tokens < bound)
    return jnp.where(keep, scores, NEGATIVE)


def stacked_heads(rows, first):
    return jnp.concatenate(
        [rows[:, (first + h) * HDIM : (first + h + 1) * HDIM] for h in range(KVHEADS)], axis=0
    )


def softmax_part(scores, values):
    highest = jnp.max(scores, axis=0, keepdims=True)
    weights = jnp.exp(scores - highest)
    total = jnp.sum(weights, axis=0, keepdims=True)
    numerator = lax.dot_general(
        weights.astype(jnp.bfloat16),
        values,
        (((0,), (0,)), ((), ())),
        preferred_element_type=jnp.float32,
    )
    return highest, total, numerator


def prompt_kernel(samples, *refs):
    query_refs, cache_ref, out_refs = refs[:samples], refs[samples], refs[samples + 1 :]
    prompts, tokens, _ = cache_ref.shape
    heads = query_refs[0].shape[1]
    marks = [[] for _ in range(samples // 2)]
    for p in range(prompts):
        rows = cache_ref[p]
        keys, values = stacked_heads(rows, 0), stacked_heads(rows, KVHEADS)
        for pair in range(samples // 2):
            query = jnp.concatenate([query_refs[2 * pair][p], query_refs[2 * pair + 1][p]], axis=0)
            scores = block_scores(keys, query, tokens, heads // KVHEADS, None)
            highest, total, numerator = softmax_part(scores, values)
            out_refs[2 * pair][p] = numerator[:heads].astype(jnp.bfloat16)
            out_refs[2 * pair + 1][p] = numerator[heads:].astype(jnp.bfloat16)
            marks[pair].append((highest, total))
    for pair, found in enumerate(marks):
        highest = jnp.concatenate([m[0] for m in found], axis=0)
        total = jnp.concatenate([m[1] for m in found], axis=0)
        rows = in_parts(highest, 3) + in_parts(total, 2)
        spare = out_refs[0].shape[0] * heads - prompts * (heads + len(rows))
        rows = rows + [jnp.zeros((spare, rows[0].shape[1]), jnp.float32)]
        slab = jnp.concatenate(rows, axis=0).astype(jnp.bfloat16)
        for i in range(slab.shape[0] // heads):
            for k in (2 * pair, 2 * pair + 1):
                out_refs[k][prompts + i] = slab[i * heads : (i + 1) * heads]


def in_parts(values, count):
    parts = []
    for _ in range(count):
        parts.append(values.astype(jnp.bfloat16).astype(jnp.float32))
        values = values - parts[-1]
    return parts


def gen_kernel(length_ref, query_ref, cache_ref, out_ref, stat_ref):
    prompts, tokens, _ = cache_ref.shape
    heads = query_ref.shape[1]
    for p in range(prompts):
        rows = cache_ref[p]
        keys, values = stacked_heads(rows, 0), stacked_heads(rows, KVHEADS)
        scores = block_scores(keys, query_ref[p], tokens, heads // KVHEADS, length_ref[p])
        highest, total, numerator = softmax_part(scores, values)
        out_ref[p] = numerator
        stat_ref[0, p : p + 1, :] = highest
        stat_ref[1, p : p + 1, :] = total


VMEM_SPEC = pl.BlockSpec(memory_space=pltpu.VMEM)
ANY_SPEC = pl.BlockSpec(memory_space=pl.ANY)
SMEM_SPEC = pl.BlockSpec(memory_space=pltpu.SMEM)


def in_hbm(array):
    return pltpu.with_memory_space_constraint(array, pltpu.HBM)


def fetch_kernel(source_ref, target_ref, sems):
    pieces = sems.shape[0]
    step = source_ref.shape[0] // pieces
    copies = [
        pltpu.make_async_copy(
            source_ref.at[pl.ds(i * step, step)], target_ref.at[pl.ds(i * step, step)], sems.at[i]
        )
        for i in range(pieces)
    ]
    for copy in copies:
        copy.start()
    for copy in copies:
        copy.wait()


def fetch(array):
    return pl.pallas_call(
        fetch_kernel,
        out_shape=jax.ShapeDtypeStruct(array.shape, array.dtype),
        in_specs=[ANY_SPEC],
        out_specs=VMEM_SPEC,
        scratch_shapes=[pltpu.SemaphoreType.DMA((math.gcd(array.shape[0], 12),))],
        compiler_params=pltpu.CompilerParams(vmem_limit_bytes=MIB),
        cost_estimate=pl.CostEstimate(flops=0, bytes_accessed=4 * array.size, transcendentals=0),
    )(in_hbm(array))


def prompt_part(queries, cache):
    samples = len(queries)
    prompts, heads, _ = queries[0].shape
    slabs = -(-5 * prompts // heads)
    return pl.pallas_call(
        functools.partial(prompt_kernel, samples),
        out_shape=[jax.ShapeDtypeStruct((prompts + slabs, heads, HDIM), jnp.bfloat16)] * samples,
        in_specs=[VMEM_SPEC] * (samples + 1),
        out_specs=[VMEM_SPEC] * samples,
        compiler_params=pltpu.CompilerParams(vmem_limit_bytes=SCOPED),
        cost_estimate=pl.CostEstimate(
            flops=1000 * 1000 * 1000, bytes_accessed=4 * MIB, transcendentals=500 * 1000
        ),
    )(*queries, cache)


def part_marks(part, prompts, k):
    heads = part.shape[1]
    slab = part[prompts:].reshape(-1, HDIM)[:, k % 2 * heads : (k % 2 + 1) * heads]
    slab = slab.astype(jnp.float32)
    rows = [slab[i * prompts : (i + 1) * prompts] for i in range(5)]
    return rows[0] + rows[1] + rows[2], rows[3] + rows[4]


def gen_part(query, cache, lengths):
    shape = query.shape
    return pl.pallas_call(
        gen_kernel,
        out_shape=[
            jax.ShapeDtypeStruct(shape, jnp.float32),
            jax.ShapeDtypeStruct((2, shape[0], shape[1]), jnp.float32),
        ],
        in_specs=[SMEM_SPEC, VMEM_SPEC, VMEM_SPEC],
        out_specs=[VMEM_SPEC, VMEM_SPEC],
        compiler_params=pltpu.CompilerParams(vmem_limit_bytes=SCOPED),
        cost_estimate=pl.CostEstimate(
            flops=100 * 1000 * 1000, bytes_accessed=2 * MIB, transcendentals=100 * 1000
        ),
    )(lengths, query, cache)


def project_kernel(samples, features, place_ref, *refs):
    attended_refs = refs[:samples]
    weight_ref, residual_ref, gain_ref, mixed_ref, row_ref, order_ref = refs[samples:]
    prompts = attended_refs[0].shape[0]
    stacked = jnp.concatenate([r[...] for r in attended_refs], axis=0)
    total = jnp.dot(stacked, weight_ref[...], preferred_element_type=jnp.float32)
    for k in range(samples):
        s = lax.rem(place_ref[0] - k + samples, samples)
        order_ref[pl.ds(pl.multiple_of(s * prompts, prompts), prompts), :] = total[
            k * prompts : (k + 1) * prompts, :
        ]
    projected = order_ref[...]
    mixed_ref[...] = projected.astype(jnp.bfloat16)
    stream = residual_ref[...].astype(jnp.float32) + projected
    square = jnp.sum(stream * stream, axis=1, keepdims=True)
    high = square.astype(jnp.bfloat16).astype(jnp.float32)
    low = square - high
    row_ref[:, :features] = (stream * gain_ref[...]).astype(jnp.bfloat16)
    lane = lax.broadcasted_iota(jnp.int32, (square.shape[0], HDIM), 1)
    row_ref[:, features:] = jnp.where(lane == 0, high, jnp.where(lane == 1, low, 0.0)).astype(
        jnp.bfloat16
    )


def project(attended, out_proj, residual, gain, place):
    samples = len(attended)
    prompts, inner = attended[0].shape
    width = out_proj.shape[1]
    rows = samples * prompts
    return pl.pallas_call(
        functools.partial(project_kernel, samples, width),
        out_shape=[
            jax.ShapeDtypeStruct((rows, width), jnp.bfloat16),
            jax.ShapeDtypeStruct((rows, width + HDIM), jnp.bfloat16),
        ],
        in_specs=[SMEM_SPEC] + [VMEM_SPEC] * (samples + 3),
        out_specs=[VMEM_SPEC] * 2,
        scratch_shapes=[pltpu.VMEM((rows, width), jnp.float32)],
        compiler_params=pltpu.CompilerParams(vmem_limit_bytes=SCOPED),
        cost_estimate=pl.CostEstimate(
            flops=2 * rows * inner * width, bytes_accessed=2 * inner * width, transcendentals=0
        ),
    )(place, *attended, out_proj, residual, gain)


def gate_kernel(
    features, expert, place_ref, pick_ref, near_ref, far_ref, extra_ref, weight_ref, *refs
):
    slots = pick_ref.shape[0]
    keep_refs, give_ref, held_ref, sems = refs[:-3], refs[-3], refs[-2], refs[-1]
    half = near_ref.shape[0]
    samples = 2 * len(keep_refs)
    hidden = weight_ref.shape[2] // 2
    part = hidden // samples
    order = list(range(1, samples, 2)) + list(range(samples - 2, -1, -2))
    copies = {}
    for m in order:
        column = lax.bitwise_xor(place_ref[0], m) * part
        for side in range(2):
            columns = pl.ds(pl.multiple_of(side * hidden + column, HDIM), part)
            copies[m, side] = pltpu.make_async_copy(
                weight_ref.at[expert, :, columns], held_ref.at[m, side], sems.at[m, side]
            )
            copies[m, side].start()
    pick = pick_ref[...]
    chosen = jnp.dot(
        pick[:, :half], near_ref[:, :features], preferred_element_type=jnp.float32
    ) + jnp.dot(pick[:, half:], far_ref[:, :features], preferred_element_type=jnp.float32)
    chosen = chosen.astype(jnp.bfloat16)
    for m in order:
        out_ref = give_ref.at[m // 2] if m % 2 else keep_refs[m // 2]
        for side in range(2):
            copies[m, side].wait()
            columns = slice(side * part, (side + 1) * part)
            share = jnp.dot(chosen, held_ref[m, side], preferred_element_type=jnp.float32)
            if out_ref.shape[0] > slots:
                share = jnp.concatenate([share, extra_ref[:, columns]], axis=0)
            out_ref[:, columns] = share.astype(jnp.bfloat16)


def gate_up_parts(pick, near, far, extra, weights, expert, place, samples):
    slots, rows = pick.shape
    more = 0 if expert else extra.shape[0]
    _, features, wide = weights.shape
    hidden = wide // 2
    part = hidden // samples
    if part % HDIM:
        chosen = jnp.dot(
            pick,
            jnp.concatenate([near, far], axis=0)[:, :features],
            preferred_element_type=jnp.float32,
        ).astype(jnp.bfloat16)
        shares = jnp.dot(chosen, weights[expert], preferred_element_type=jnp.float32)
        shares = shares.astype(jnp.bfloat16).reshape(slots, 2, samples, part)
        wanted = (jnp.bitwise_xor(place[0], jnp.arange(samples))[:, None] == jnp.arange(samples)).astype(
            jnp.bfloat16
        )
        shares = jnp.einsum("mn,sgnp->msgp", wanted, shares, preferred_element_type=jnp.float32)
        shares = shares.astype(jnp.bfloat16).reshape(samples, slots, 2 * part)
        behind = jnp.broadcast_to(extra.astype(jnp.bfloat16)[:more], (samples, more, 2 * part))
        shares = jnp.concatenate([shares, behind], axis=1)
        return [shares[m] for m in range(0, samples, 2)], shares[1::2]
    one = jax.ShapeDtypeStruct((slots + more, 2 * part), jnp.bfloat16)
    results = pl.pallas_call(
        functools.partial(gate_kernel, features, expert),
        out_shape=[one] * (samples // 2)
        + [jax.ShapeDtypeStruct((samples // 2, slots + more, 2 * part), jnp.bfloat16)],
        in_specs=[SMEM_SPEC] + [VMEM_SPEC] * 4 + [ANY_SPEC],
        out_specs=[VMEM_SPEC] * (samples // 2 + 1),
        scratch_shapes=[
            pltpu.VMEM((samples, 2, features, part), jnp.bfloat16),
            pltpu.SemaphoreType.DMA((samples, 2)),
        ],
        compiler_params=pltpu.CompilerParams(vmem_limit_bytes=SCOPED + 2 * features * wide),
        cost_estimate=pl.CostEstimate(
            flops=2 * slots * features * wide, bytes_accessed=2 * features * wide, transcendentals=0
        ),
    )(place, pick, near, far, extra, in_hbm(weights))
    return results[:-1], results[-1]


def reduce_parts(keep, arrived, samples):
    bits = 1
    while True:
        keep = [a.astype(jnp.float32) + arrived[i].astype(jnp.float32) for i, a in enumerate(keep)]
        bits *= 2
        if bits == samples:
            return keep[0]
        arrived = swap(
            jnp.stack([a.astype(jnp.bfloat16) for a in keep[1::2]]), "sample", samples, bits
        )
        keep = keep[0::2]


def gather_parts(act, samples):
    held, order, bits = [act], [0], samples // 2
    while bits > 1:
        arrived = swap(jnp.stack(held), "sample", samples, bits)
        held = held + [arrived[i] for i in range(len(held))]
        order = order + [m + bits for m in order]
        bits //= 2
    near = jnp.stack(held)
    return near, swap(near, "sample", samples, 1), order


def down_kernel(order, place_ref, *refs):
    pick_ref, weight_ref, near_out_ref, far_out_ref = refs[-4:]
    experts = weight_ref.shape[0]
    part = refs[0].shape[2]
    half = near_out_ref.shape[0]
    near_sum = far_sum = None
    for j in range(experts):
        total = None
        for n, m in enumerate(order):
            for odd in range(2):
                row = pl.multiple_of(lax.bitwise_xor(place_ref[0], m + odd) * part, HDIM)
                share = jnp.dot(
                    refs[2 * j + odd][n], weight_ref[j, pl.ds(row, part)], preferred_element_type=jnp.float32
                )
                total = share if total is None else total + share
        finished = total.astype(jnp.bfloat16)
        given = lax.dot_general(
            pick_ref[j], finished, (((0,), (0,)), ((), ())), preferred_element_type=jnp.float32
        )
        near_sum = given[:half] if near_sum is None else near_sum + given[:half]
        far_sum = given[half:] if far_sum is None else far_sum + given[half:]
    near_out_ref[...] = near_sum
    far_out_ref[...] = far_sum.astype(jnp.bfloat16)


def down_rows(acts, order, pick, weights, place):
    pairs, slots, part = acts[0].shape
    experts, hidden, width = weights.shape
    half = pick.shape[2] // 2
    shapes = [
        jax.ShapeDtypeStruct((half, width), jnp.float32),
        jax.ShapeDtypeStruct((half, width), jnp.bfloat16),
    ]
    if part % HDIM:
        known = jnp.array(order + [m + 1 for m in order], jnp.int32)
        held = jnp.bitwise_xor(place[0], known)[None, :] == jnp.arange(2 * pairs)[:, None]
        total = jnp.zeros((2 * half, width), jnp.float32)
        for j in range(experts):
            joined = jnp.einsum(
                "ni,isp->snp",
                held.astype(jnp.bfloat16),
                jnp.concatenate(acts[2 * j : 2 * j + 2], axis=0),
                preferred_element_type=jnp.float32,
            )
            joined = joined.astype(jnp.bfloat16).reshape(slots, hidden)
            finished = jnp.dot(joined, weights[j], preferred_element_type=jnp.float32)
            total = total + lax.dot_general(
                pick[j],
                finished.astype(jnp.bfloat16),
                (((0,), (0,)), ((), ())),
                preferred_element_type=jnp.float32,
            )
        return total[:half], total[half:].astype(jnp.bfloat16)
    return pl.pallas_call(
        functools.partial(down_kernel, order),
        out_shape=shapes,
        in_specs=[SMEM_SPEC] + [VMEM_SPEC] * (2 * experts + 1) + [VMEM_SPEC],
        out_specs=[VMEM_SPEC] * 2,
        compiler_params=pltpu.CompilerParams(vmem_limit_bytes=SCOPED),
        cost_estimate=pl.CostEstimate(
            flops=2 * experts * slots * hidden * width,
            bytes_accessed=2 * experts * hidden * width,
            transcendentals=0,
        ),
    )(place, *acts, pick, weights)


def gather_experts(array, owners):
    near = jnp.concatenate(
        [array] + [swap(array, "expert", owners, b) for b in range(2, owners, 2)], axis=0
    )
    return near, swap(near, "expert", owners, 1)


def on_device(
    queries,
    prompt_kv,
    gen_kv,
    gen_lengths,
    out_proj,
    residual,
    norm_gain,
    w_gate_up,
    w_down,
    routes,
    route_probs,
):
    samples, owners = lax.axis_size("sample"), lax.axis_size("expert")
    place = lax.axis_index("sample").astype(jnp.int32).reshape(1)
    prompts = queries.shape[0]
    heads = queries.shape[2] // HDIM
    width = residual.shape[2]
    rows = prompts * samples
    per_owner = w_gate_up.shape[0]
    hidden = w_down.shape[1]

    query = queries.reshape(prompts, heads, HDIM)
    all_queries = [query] + [send(query, "sample", samples, k) for k in range(1, samples)]

    gen_out, gen_stat = gen_part(query, gen_kv[:, 0], gen_lengths[:, 0])
    routes, route_probs, gen_out = lax.optimization_barrier((routes, route_probs, gen_out))
    by_sample = lambda a: jnp.swapaxes(a, 0, 1).reshape(rows, TOPK)
    table = jnp.concatenate(
        [by_sample(routes).astype(jnp.float32), by_sample(route_probs)], axis=1
    )
    table = jnp.concatenate(gather_experts(table, owners), axis=0)
    capacity = 5 * rows * TOPK // (4 * per_owner * owners)
    slots = owners * capacity
    first = lax.axis_index("expert") * per_owner
    mine = (first + jnp.arange(per_owner, dtype=jnp.int32)).astype(jnp.float32)
    match = table[None, :, :TOPK] == mine[:, None, None]
    hit = jnp.any(match, axis=2)
    weight = jnp.sum(jnp.where(match, table[None, :, TOPK:], 0.0), axis=2)
    hit_blocks = hit.reshape(per_owner, owners, rows)
    earlier = (jnp.arange(rows)[:, None] < jnp.arange(rows)[None, :]).astype(jnp.bfloat16)
    rank = jnp.einsum(
        "jbr,rq->jbq",
        hit_blocks.astype(jnp.bfloat16),
        earlier,
        preferred_element_type=jnp.float32,
    ).astype(jnp.int32)
    slot = rank + capacity * jnp.arange(owners, dtype=jnp.int32)[None, :, None]
    slot = jnp.where(hit_blocks, slot, -1).reshape(per_owner, owners * rows)
    chosen = slot[:, None, :] == jnp.arange(slots, dtype=jnp.int32)[None, :, None]
    pick = chosen.astype(jnp.bfloat16)
    slot_weight = jnp.sum(jnp.where(chosen, weight[:, None, :], 0.0), axis=2)

    parts = list(prompt_part(all_queries, prompt_kv))
    parts = [parts[0]] + [send(parts[k], "sample", samples, -k) for k in range(1, samples)]
    outs = [gen_out] + [part[:prompts] for part in parts]
    marks = [(gen_stat[0], gen_stat[1])] + [
        part_marks(part, prompts, k) for k, part in enumerate(parts)
    ]
    highest = functools.reduce(jnp.maximum, [m[0] for m in marks])
    scales = [jnp.exp(m[0] - highest) for m in marks]
    total = sum(c * m[1] for c, m in zip(scales, marks))
    attended = sum(
        o.astype(jnp.float32) * (c / total)[:, :, None] for o, c in zip(outs, scales)
    )
    attended = attended.astype(jnp.bfloat16).reshape(prompts, heads * HDIM)
    out_proj, attended = lax.optimization_barrier((out_proj, attended))
    out_proj = fetch(out_proj)
    attended = [attended] + [send(attended, "sample", samples, k) for k in range(1, samples)]
    mixed, row_block = project(
        attended,
        out_proj,
        jnp.swapaxes(residual, 0, 1).reshape(rows, width),
        norm_gain.reshape(1, width),
        place,
    )
    mixed = jnp.swapaxes(mixed.reshape(samples, prompts, width), 0, 1)

    near, far = gather_experts(row_block, owners)
    part = hidden // samples
    square = jnp.concatenate([near[:, width : width + 2], far[:, width : width + 2]], axis=0)
    square = square.astype(jnp.float32).T.reshape(-1)
    total_rows = owners * rows
    extra_rows = -(-2 * total_rows // (16 * part)) * 8
    extra = jnp.pad(square, (0, extra_rows * 2 * part - square.size)).reshape(extra_rows, 2 * part)
    sums = []
    for j in range(per_owner):
        keep, give = gate_up_parts(pick[j], near, far, extra, w_gate_up, j, place, samples)
        arrived = swap(give, "sample", samples, 1)
        sums.append((keep, arrived))
    acts = []
    for j in range(per_owner):
        gate_up = reduce_parts(*sums[j], samples)
        if j == 0:
            square = gate_up[slots:].reshape(-1)
            square = square[:total_rows] + square[total_rows : 2 * total_rows]
            factor = lax.rsqrt(square / (width * samples) + EPSILON)
            slot_factor = jnp.sum(jnp.where(chosen, factor[None, None, :], 0.0), axis=2)
            gate_up = gate_up[:slots]
        gate_up = gate_up * slot_factor[j][:, None]
        act = jax.nn.silu(gate_up[:, :part]) * gate_up[:, part:] * slot_weight[j][:, None]
        act = act.astype(jnp.bfloat16)
        act_near, act_far, order = gather_parts(act, samples)
        acts = acts + [act_near, act_far]
    w_down, acts[-2] = lax.optimization_barrier((w_down, acts[-2]))
    w_down = fetch(w_down)
    kept, given = down_rows(acts, order, pick, w_down, place)
    kept = kept.reshape(owners // 2, rows, width)
    arrived = swap(given.reshape(owners // 2, rows, width), "expert", owners, 1)
    paired = kept + arrived.astype(jnp.float32)
    outgoing = paired.astype(jnp.bfloat16)
    combined = paired[0]
    for b in range(1, owners // 2):
        combined = combined + swap(outgoing[b], "expert", owners, 2 * b).astype(jnp.float32)
    expert_out = combined.astype(jnp.bfloat16).reshape(samples, prompts, width)
    return mixed, jnp.swapaxes(expert_out, 0, 1)


def solution(mesh):
    placed = (
        P("expert", "sample", None),
        P("expert", "sample", None),
        P("expert", "sample", None, None),
        P("expert", "sample"),
        P(None, "sample"),
        P("expert", None, "sample"),
        P("sample"),
        P("expert", "sample", None),
        P("expert", None, "sample"),
        P("expert", None, None),
        P("expert", None, None),
    )
    return jax.shard_map(
        on_device,
        mesh=mesh,
        in_specs=placed,
        out_specs=(P("expert", None, "sample"), P("expert", None, "sample")),
        check_vma=False,
    )
```

```python
import functools
import math

import jax
import jax.numpy as jnp
from jax import lax
from jax.experimental import pallas as pl
from jax.experimental.pallas import tpu as pltpu
from jax.sharding import PartitionSpec as P

KVHEADS = 4
HDIM = 128
TOPK = 8
NEGATIVE = -1e30
EPSILON = 1e-06
CARRIER = 0
MIB = 1 << 20
SCOPED = 10 * MIB


def send(array, axis, size, shift):
    return lax.ppermute(array, axis, [(i, (i + shift) % size) for i in range(size)])


def swap(array, axis, size, bits):
    return lax.ppermute(array, axis, [(i, i ^ bits) for i in range(size)])


def block_scores(keys, query, tokens, groups, bound):
    scores = lax.dot_general(
        keys, query, (((1,), (1,)), ((), ())), preferred_element_type=jnp.float32
    ) * (HDIM**-0.5)
    row = lax.broadcasted_iota(jnp.int32, scores.shape, 0)
    lane = lax.broadcasted_iota(jnp.int32, scores.shape, 1)
    keep = row // tokens == (lane // groups) % KVHEADS
    if bound is not None:
        keep = keep & (row % tokens < bound)
    return jnp.where(keep, scores, NEGATIVE)


def stacked_heads(rows, first):
    return jnp.concatenate(
        [rows[:, (first + h) * HDIM : (first + h + 1) * HDIM] for h in range(KVHEADS)], axis=0
    )


def softmax_part(scores, values):
    highest = jnp.max(scores, axis=0, keepdims=True)
    weights = jnp.exp(scores - highest)
    total = jnp.sum(weights, axis=0, keepdims=True)
    numerator = lax.dot_general(
        weights.astype(jnp.bfloat16),
        values,
        (((0,), (0,)), ((), ())),
        preferred_element_type=jnp.float32,
    )
    return highest, total, numerator


def prompt_kernel(samples, *refs):
    query_refs, cache_ref, out_refs = refs[:samples], refs[samples], refs[samples + 1 :]
    prompts, tokens, _ = cache_ref.shape
    heads = query_refs[0].shape[1]
    marks = [[] for _ in range(samples // 2)]
    for p in range(prompts):
        rows = cache_ref[p]
        keys, values = stacked_heads(rows, 0), stacked_heads(rows, KVHEADS)
        for pair in range(samples // 2):
            query = jnp.concatenate([query_refs[2 * pair][p], query_refs[2 * pair + 1][p]], axis=0)
            scores = block_scores(keys, query, tokens, heads // KVHEADS, None)
            highest, total, numerator = softmax_part(scores, values)
            out_refs[2 * pair][p] = numerator[:heads].astype(jnp.bfloat16)
            out_refs[2 * pair + 1][p] = numerator[heads:].astype(jnp.bfloat16)
            marks[pair].append((highest, total))
    for pair, found in enumerate(marks):
        highest = jnp.concatenate([m[0] for m in found], axis=0)
        total = jnp.concatenate([m[1] for m in found], axis=0)
        rows = in_parts(highest, 3) + in_parts(total, 2)
        spare = out_refs[0].shape[0] * heads - prompts * (heads + len(rows))
        rows = rows + [jnp.zeros((spare, rows[0].shape[1]), jnp.float32)]
        slab = jnp.concatenate(rows, axis=0).astype(jnp.bfloat16)
        for i in range(slab.shape[0] // heads):
            for k in (2 * pair, 2 * pair + 1):
                out_refs[k][prompts + i] = slab[i * heads : (i + 1) * heads]


def in_parts(values, count):
    parts = []
    for _ in range(count):
        parts.append(values.astype(jnp.bfloat16).astype(jnp.float32))
        values = values - parts[-1]
    return parts


def gen_kernel(length_ref, query_ref, cache_ref, out_ref, stat_ref):
    prompts, tokens, _ = cache_ref.shape
    heads = query_ref.shape[1]
    for p in range(prompts):
        rows = cache_ref[p]
        keys, values = stacked_heads(rows, 0), stacked_heads(rows, KVHEADS)
        scores = block_scores(keys, query_ref[p], tokens, heads // KVHEADS, length_ref[p])
        highest, total, numerator = softmax_part(scores, values)
        out_ref[p] = numerator
        stat_ref[0, p : p + 1, :] = highest
        stat_ref[1, p : p + 1, :] = total


VMEM_SPEC = pl.BlockSpec(memory_space=pltpu.VMEM)
ANY_SPEC = pl.BlockSpec(memory_space=pl.ANY)
SMEM_SPEC = pl.BlockSpec(memory_space=pltpu.SMEM)


def in_hbm(array):
    return pltpu.with_memory_space_constraint(array, pltpu.HBM)


def fetch_kernel(source_ref, target_ref, sems):
    pieces = sems.shape[0]
    step = source_ref.shape[0] // pieces
    copies = [
        pltpu.make_async_copy(
            source_ref.at[pl.ds(i * step, step)], target_ref.at[pl.ds(i * step, step)], sems.at[i]
        )
        for i in range(pieces)
    ]
    for copy in copies:
        copy.start()
    for copy in copies:
        copy.wait()


def fetch(array):
    return pl.pallas_call(
        fetch_kernel,
        out_shape=jax.ShapeDtypeStruct(array.shape, array.dtype),
        in_specs=[ANY_SPEC],
        out_specs=VMEM_SPEC,
        scratch_shapes=[pltpu.SemaphoreType.DMA((math.gcd(array.shape[0], 12),))],
        compiler_params=pltpu.CompilerParams(vmem_limit_bytes=MIB),
        cost_estimate=pl.CostEstimate(flops=0, bytes_accessed=4 * array.size, transcendentals=0),
    )(in_hbm(array))


def prompt_part(queries, cache):
    samples = len(queries)
    prompts, heads, _ = queries[0].shape
    slabs = -(-5 * prompts // heads)
    return pl.pallas_call(
        functools.partial(prompt_kernel, samples),
        out_shape=[jax.ShapeDtypeStruct((prompts + slabs, heads, HDIM), jnp.bfloat16)] * samples,
        in_specs=[VMEM_SPEC] * (samples + 1),
        out_specs=[VMEM_SPEC] * samples,
        compiler_params=pltpu.CompilerParams(vmem_limit_bytes=SCOPED),
        cost_estimate=pl.CostEstimate(
            flops=1000 * 1000 * 1000, bytes_accessed=4 * MIB, transcendentals=500 * 1000
        ),
    )(*queries, cache)


def part_marks(part, prompts, k):
    heads = part.shape[1]
    slab = part[prompts:].reshape(-1, HDIM)[:, k % 2 * heads : (k % 2 + 1) * heads]
    slab = slab.astype(jnp.float32)
    rows = [slab[i * prompts : (i + 1) * prompts] for i in range(5)]
    return rows[0] + rows[1] + rows[2], rows[3] + rows[4]


def gen_part(query, cache, lengths):
    shape = query.shape
    return pl.pallas_call(
        gen_kernel,
        out_shape=[
            jax.ShapeDtypeStruct(shape, jnp.float32),
            jax.ShapeDtypeStruct((2, shape[0], shape[1]), jnp.float32),
        ],
        in_specs=[SMEM_SPEC, VMEM_SPEC, VMEM_SPEC],
        out_specs=[VMEM_SPEC, VMEM_SPEC],
        compiler_params=pltpu.CompilerParams(vmem_limit_bytes=SCOPED),
        cost_estimate=pl.CostEstimate(
            flops=100 * 1000 * 1000, bytes_accessed=2 * MIB, transcendentals=100 * 1000
        ),
    )(lengths, query, cache)


def project_kernel(samples, features, place_ref, *refs):
    attended_refs = refs[:samples]
    weight_ref, residual_ref, gain_ref, mixed_ref, row_ref, order_ref = refs[samples:]
    prompts = attended_refs[0].shape[0]
    stacked = jnp.concatenate([r[...] for r in attended_refs], axis=0)
    total = jnp.dot(stacked, weight_ref[...], preferred_element_type=jnp.float32)
    for k in range(samples):
        s = lax.rem(place_ref[0] - k + samples, samples)
        order_ref[pl.ds(pl.multiple_of(s * prompts, prompts), prompts), :] = total[
            k * prompts : (k + 1) * prompts, :
        ]
    projected = order_ref[...]
    mixed_ref[...] = projected.astype(jnp.bfloat16)
    stream = residual_ref[...].astype(jnp.float32) + projected
    square = jnp.sum(stream * stream, axis=1, keepdims=True)
    high = square.astype(jnp.bfloat16).astype(jnp.float32)
    low = square - high
    row_ref[:, :features] = (stream * gain_ref[...]).astype(jnp.bfloat16)
    lane = lax.broadcasted_iota(jnp.int32, (square.shape[0], HDIM), 1)
    row_ref[:, features:] = jnp.where(lane == 0, high, jnp.where(lane == 1, low, 0.0)).astype(
        jnp.bfloat16
    )


def project(attended, out_proj, residual, gain, place):
    samples = len(attended)
    prompts, inner = attended[0].shape
    width = out_proj.shape[1]
    rows = samples * prompts
    return pl.pallas_call(
        functools.partial(project_kernel, samples, width),
        out_shape=[
            jax.ShapeDtypeStruct((rows, width), jnp.bfloat16),
            jax.ShapeDtypeStruct((rows, width + HDIM), jnp.bfloat16),
        ],
        in_specs=[SMEM_SPEC] + [VMEM_SPEC] * (samples + 3),
        out_specs=[VMEM_SPEC] * 2,
        scratch_shapes=[pltpu.VMEM((rows, width), jnp.float32)],
        compiler_params=pltpu.CompilerParams(vmem_limit_bytes=SCOPED),
        cost_estimate=pl.CostEstimate(
            flops=2 * rows * inner * width, bytes_accessed=2 * inner * width, transcendentals=0
        ),
    )(place, *attended, out_proj, residual, gain)


def gate_kernel(
    features, expert, place_ref, pick_ref, near_ref, far_ref, extra_ref, weight_ref, *refs
):
    slots = pick_ref.shape[0]
    keep_refs, give_ref, held_ref, sems = refs[:-3], refs[-3], refs[-2], refs[-1]
    half = near_ref.shape[0]
    samples = 2 * len(keep_refs)
    hidden = weight_ref.shape[2] // 2
    part = hidden // samples
    order = list(range(1, samples, 2)) + list(range(samples - 2, -1, -2))
    copies = {}
    for m in order:
        column = lax.bitwise_xor(place_ref[0], m) * part
        for side in range(2):
            columns = pl.ds(pl.multiple_of(side * hidden + column, HDIM), part)
            copies[m, side] = pltpu.make_async_copy(
                weight_ref.at[expert, :, columns], held_ref.at[m, side], sems.at[m, side]
            )
            copies[m, side].start()
    pick = pick_ref[...]
    chosen = jnp.dot(
        pick[:, :half], near_ref[:, :features], preferred_element_type=jnp.float32
    ) + jnp.dot(pick[:, half:], far_ref[:, :features], preferred_element_type=jnp.float32)
    chosen = chosen.astype(jnp.bfloat16)
    for m in order:
        out_ref = give_ref.at[m // 2] if m % 2 else keep_refs[m // 2]
        for side in range(2):
            copies[m, side].wait()
            columns = slice(side * part, (side + 1) * part)
            share = jnp.dot(chosen, held_ref[m, side], preferred_element_type=jnp.float32)
            if out_ref.shape[0] > slots:
                share = jnp.concatenate([share, extra_ref[:, columns]], axis=0)
            out_ref[:, columns] = share.astype(jnp.bfloat16)


def gate_up_parts(pick, near, far, extra, weights, expert, place, samples):
    slots, rows = pick.shape
    more = extra.shape[0] if expert == CARRIER else 0
    _, features, wide = weights.shape
    hidden = wide // 2
    part = hidden // samples
    if part % HDIM:
        chosen = jnp.dot(
            pick,
            jnp.concatenate([near, far], axis=0)[:, :features],
            preferred_element_type=jnp.float32,
        ).astype(jnp.bfloat16)
        shares = jnp.dot(chosen, weights[expert], preferred_element_type=jnp.float32)
        shares = shares.astype(jnp.bfloat16).reshape(slots, 2, samples, part)
        wanted = (jnp.bitwise_xor(place[0], jnp.arange(samples))[:, None] == jnp.arange(samples)).astype(
            jnp.bfloat16
        )
        shares = jnp.einsum("mn,sgnp->msgp", wanted, shares, preferred_element_type=jnp.float32)
        shares = shares.astype(jnp.bfloat16).reshape(samples, slots, 2 * part)
        behind = jnp.broadcast_to(extra.astype(jnp.bfloat16)[:more], (samples, more, 2 * part))
        shares = jnp.concatenate([shares, behind], axis=1)
        return [shares[m] for m in range(0, samples, 2)], shares[1::2]
    one = jax.ShapeDtypeStruct((slots + more, 2 * part), jnp.bfloat16)
    results = pl.pallas_call(
        functools.partial(gate_kernel, features, expert),
        out_shape=[one] * (samples // 2)
        + [jax.ShapeDtypeStruct((samples // 2, slots + more, 2 * part), jnp.bfloat16)],
        in_specs=[SMEM_SPEC] + [VMEM_SPEC] * 4 + [ANY_SPEC],
        out_specs=[VMEM_SPEC] * (samples // 2 + 1),
        scratch_shapes=[
            pltpu.VMEM((samples, 2, features, part), jnp.bfloat16),
            pltpu.SemaphoreType.DMA((samples, 2)),
        ],
        compiler_params=pltpu.CompilerParams(vmem_limit_bytes=SCOPED + 2 * features * wide),
        cost_estimate=pl.CostEstimate(
            flops=2 * slots * features * wide, bytes_accessed=2 * features * wide, transcendentals=0
        ),
    )(place, pick, near, far, extra, in_hbm(weights))
    return results[:-1], results[-1]


def reduce_parts(keep, arrived, samples, after):
    bits = 1
    while True:
        keep = [a.astype(jnp.float32) + arrived[i].astype(jnp.float32) for i, a in enumerate(keep)]
        bits *= 2
        if bits == samples:
            return keep[0]
        give = jnp.stack([a.astype(jnp.bfloat16) for a in keep[1::2]])
        if after is not None:
            give, _ = lax.optimization_barrier((give, after))
        arrived = swap(give, "sample", samples, bits)
        keep = keep[0::2]


def gather_parts(act, samples):
    held, order, bits = [act], [0], samples // 2
    while bits > 1:
        arrived = swap(jnp.stack(held), "sample", samples, bits)
        held = held + [arrived[i] for i in range(len(held))]
        order = order + [m + bits for m in order]
        bits //= 2
    near = jnp.stack(held)
    return near, swap(near, "sample", samples, 1), order


def down_kernel(order, place_ref, *refs):
    pick_ref, weight_ref, near_out_ref, far_out_ref = refs[-4:]
    experts = weight_ref.shape[0]
    part = refs[0].shape[2]
    half = near_out_ref.shape[0]
    near_sum = far_sum = None
    for j in range(experts):
        total = None
        for n, m in enumerate(order):
            for odd in range(2):
                row = pl.multiple_of(lax.bitwise_xor(place_ref[0], m + odd) * part, HDIM)
                share = jnp.dot(
                    refs[2 * j + odd][n], weight_ref[j, pl.ds(row, part)], preferred_element_type=jnp.float32
                )
                total = share if total is None else total + share
        finished = total.astype(jnp.bfloat16)
        given = lax.dot_general(
            pick_ref[j], finished, (((0,), (0,)), ((), ())), preferred_element_type=jnp.float32
        )
        near_sum = given[:half] if near_sum is None else near_sum + given[:half]
        far_sum = given[half:] if far_sum is None else far_sum + given[half:]
    near_out_ref[...] = near_sum
    far_out_ref[...] = far_sum.astype(jnp.bfloat16)


def down_rows(acts, order, pick, weights, place):
    pairs, slots, part = acts[0].shape
    experts, hidden, width = weights.shape
    half = pick.shape[2] // 2
    shapes = [
        jax.ShapeDtypeStruct((half, width), jnp.float32),
        jax.ShapeDtypeStruct((half, width), jnp.bfloat16),
    ]
    if part % HDIM:
        known = jnp.array(order + [m + 1 for m in order], jnp.int32)
        held = jnp.bitwise_xor(place[0], known)[None, :] == jnp.arange(2 * pairs)[:, None]
        total = jnp.zeros((2 * half, width), jnp.float32)
        for j in range(experts):
            joined = jnp.einsum(
                "ni,isp->snp",
                held.astype(jnp.bfloat16),
                jnp.concatenate(acts[2 * j : 2 * j + 2], axis=0),
                preferred_element_type=jnp.float32,
            )
            joined = joined.astype(jnp.bfloat16).reshape(slots, hidden)
            finished = jnp.dot(joined, weights[j], preferred_element_type=jnp.float32)
            total = total + lax.dot_general(
                pick[j],
                finished.astype(jnp.bfloat16),
                (((0,), (0,)), ((), ())),
                preferred_element_type=jnp.float32,
            )
        return total[:half], total[half:].astype(jnp.bfloat16)
    return pl.pallas_call(
        functools.partial(down_kernel, order),
        out_shape=shapes,
        in_specs=[SMEM_SPEC] + [VMEM_SPEC] * (2 * experts + 1) + [VMEM_SPEC],
        out_specs=[VMEM_SPEC] * 2,
        compiler_params=pltpu.CompilerParams(vmem_limit_bytes=SCOPED),
        cost_estimate=pl.CostEstimate(
            flops=2 * experts * slots * hidden * width,
            bytes_accessed=2 * experts * hidden * width,
            transcendentals=0,
        ),
    )(place, *acts, pick, weights)


def gather_experts(array, owners):
    near = jnp.concatenate(
        [array] + [swap(array, "expert", owners, b) for b in range(2, owners, 2)], axis=0
    )
    return near, swap(near, "expert", owners, 1)


def on_device(
    queries,
    prompt_kv,
    gen_kv,
    gen_lengths,
    out_proj,
    residual,
    norm_gain,
    w_gate_up,
    w_down,
    routes,
    route_probs,
):
    samples, owners = lax.axis_size("sample"), lax.axis_size("expert")
    place = lax.axis_index("sample").astype(jnp.int32).reshape(1)
    prompts = queries.shape[0]
    heads = queries.shape[2] // HDIM
    width = residual.shape[2]
    rows = prompts * samples
    per_owner = w_gate_up.shape[0]
    hidden = w_down.shape[1]

    query = queries.reshape(prompts, heads, HDIM)
    all_queries = [query] + [send(query, "sample", samples, k) for k in range(1, samples)]

    gen_out, gen_stat = gen_part(query, gen_kv[:, 0], gen_lengths[:, 0])
    prompt_kv, _ = lax.optimization_barrier((prompt_kv, gen_out))
    parts = list(prompt_part(all_queries, fetch(prompt_kv)))
    parts = [parts[0]] + [send(parts[k], "sample", samples, -k) for k in range(1, samples)]
    routes, route_probs, parts[-1] = lax.optimization_barrier((routes, route_probs, parts[-1]))
    by_sample = lambda a: jnp.swapaxes(a, 0, 1).reshape(rows, TOPK)
    table = jnp.concatenate(
        [by_sample(routes).astype(jnp.float32), by_sample(route_probs)], axis=1
    )
    table = jnp.concatenate(gather_experts(table, owners), axis=0)
    capacity = 5 * rows * TOPK // (4 * per_owner * owners)
    slots = owners * capacity
    first = lax.axis_index("expert") * per_owner
    mine = (first + jnp.arange(per_owner, dtype=jnp.int32)).astype(jnp.float32)
    match = table[None, :, :TOPK] == mine[:, None, None]
    hit = jnp.any(match, axis=2)
    weight = jnp.sum(jnp.where(match, table[None, :, TOPK:], 0.0), axis=2)
    hit_blocks = hit.reshape(per_owner, owners, rows)
    earlier = (jnp.arange(rows)[:, None] < jnp.arange(rows)[None, :]).astype(jnp.bfloat16)
    rank = jnp.einsum(
        "jbr,rq->jbq",
        hit_blocks.astype(jnp.bfloat16),
        earlier,
        preferred_element_type=jnp.float32,
    ).astype(jnp.int32)
    slot = rank + capacity * jnp.arange(owners, dtype=jnp.int32)[None, :, None]
    slot = jnp.where(hit_blocks, slot, -1).reshape(per_owner, owners * rows)
    chosen = slot[:, None, :] == jnp.arange(slots, dtype=jnp.int32)[None, :, None]
    pick = chosen.astype(jnp.bfloat16)
    slot_weight = jnp.sum(jnp.where(chosen, weight[:, None, :], 0.0), axis=2)

    outs = [gen_out] + [part[:prompts] for part in parts]
    marks = [(gen_stat[0], gen_stat[1])] + [
        part_marks(part, prompts, k) for k, part in enumerate(parts)
    ]
    highest = functools.reduce(jnp.maximum, [m[0] for m in marks])
    scales = [jnp.exp(m[0] - highest) for m in marks]
    total = sum(c * m[1] for c, m in zip(scales, marks))
    attended = sum(
        o.astype(jnp.float32) * (c / total)[:, :, None] for o, c in zip(outs, scales)
    )
    attended = attended.astype(jnp.bfloat16).reshape(prompts, heads * HDIM)
    out_proj, _, pick, chosen, slot_weight = lax.optimization_barrier(
        (out_proj, attended, pick, chosen, slot_weight)
    )
    out_proj = fetch(out_proj)
    attended = [attended] + [send(attended, "sample", samples, k) for k in range(1, samples)]
    mixed, row_block = project(
        attended,
        out_proj,
        jnp.swapaxes(residual, 0, 1).reshape(rows, width),
        norm_gain.reshape(1, width),
        place,
    )
    mixed = jnp.swapaxes(mixed.reshape(samples, prompts, width), 0, 1)

    near, far = gather_experts(row_block, owners)
    part = hidden // samples
    square = jnp.concatenate([near[:, width : width + 2], far[:, width : width + 2]], axis=0)
    square = square.astype(jnp.float32).T.reshape(-1)
    total_rows = owners * rows
    extra_rows = -(-2 * total_rows // (16 * part)) * 8
    extra = jnp.pad(square, (0, extra_rows * 2 * part - square.size)).reshape(extra_rows, 2 * part)
    sums = {}
    for j in reversed(range(per_owner)):
        keep, give = gate_up_parts(pick[j], near, far, extra, w_gate_up, j, place, samples)
        arrived = swap(give, "sample", samples, 1)
        sums[j] = keep, arrived
    acts = [None] * (2 * per_owner)
    for j in [CARRIER] + [j for j in range(per_owner) if j != CARRIER]:
        gate_up = reduce_parts(*sums[j], samples, first_act if j == 1 else None)
        if j == CARRIER:
            square = gate_up[slots:].reshape(-1)
            square = square[:total_rows] + square[total_rows : 2 * total_rows]
            factor = lax.rsqrt(square / (width * samples) + EPSILON)
            slot_factor = jnp.sum(jnp.where(chosen, factor[None, None, :], 0.0), axis=2)
            gate_up = gate_up[:slots]
        gate_up = gate_up * slot_factor[j][:, None]
        act = jax.nn.silu(gate_up[:, :part]) * gate_up[:, part:] * slot_weight[j][:, None]
        act = act.astype(jnp.bfloat16)
        first_act = act if j == 0 else first_act
        act_near, act_far, order = gather_parts(act, samples)
        acts[2 * j : 2 * j + 2] = act_near, act_far
    w_down, acts[-2] = lax.optimization_barrier((w_down, acts[-2]))
    w_down = fetch(w_down)
    kept, given = down_rows(acts, order, pick, w_down, place)
    kept = kept.reshape(owners // 2, rows, width)
    arrived = swap(given.reshape(owners // 2, rows, width), "expert", owners, 1)
    paired = kept + arrived.astype(jnp.float32)
    outgoing = paired.astype(jnp.bfloat16)
    combined = paired[0]
    for b in range(1, owners // 2):
        combined = combined + swap(outgoing[b], "expert", owners, 2 * b).astype(jnp.float32)
    expert_out = combined.astype(jnp.bfloat16).reshape(samples, prompts, width)
    return mixed, jnp.swapaxes(expert_out, 0, 1)


def solution(mesh):
    placed = (
        P("expert", "sample", None),
        P("expert", "sample", None),
        P("expert", "sample", None, None),
        P("expert", "sample"),
        P(None, "sample"),
        P("expert", None, "sample"),
        P("sample"),
        P("expert", "sample", None),
        P("expert", None, "sample"),
        P("expert", None, None),
        P("expert", None, None),
    )
    return jax.shard_map(
        on_device,
        mesh=mesh,
        in_specs=placed,
        out_specs=(P("expert", None, "sample"), P("expert", None, "sample")),
        check_vma=False,
    )
```

```python
import functools
import math

import jax
import jax.numpy as jnp
from jax import lax
from jax.experimental import pallas as pl
from jax.experimental.pallas import tpu as pltpu
from jax.sharding import PartitionSpec as P

KVHEADS = 4
HDIM = 128
TOPK = 8
NEGATIVE = -1e30
EPSILON = 1e-06
CARRIER = 0
MIB = 1 << 20
SCOPED = 10 * MIB


def send(array, axis, size, shift):
    return lax.ppermute(array, axis, [(i, (i + shift) % size) for i in range(size)])


def swap(array, axis, size, bits):
    return lax.ppermute(array, axis, [(i, i ^ bits) for i in range(size)])


def block_scores(keys, query, tokens, groups, bound):
    scores = lax.dot_general(
        keys, query, (((1,), (1,)), ((), ())), preferred_element_type=jnp.float32
    ) * (HDIM**-0.5)
    row = lax.broadcasted_iota(jnp.int32, scores.shape, 0)
    lane = lax.broadcasted_iota(jnp.int32, scores.shape, 1)
    keep = row // tokens == (lane // groups) % KVHEADS
    if bound is not None:
        keep = keep & (row % tokens < bound)
    return jnp.where(keep, scores, NEGATIVE)


def stacked_heads(rows, first):
    return jnp.concatenate(
        [rows[:, (first + h) * HDIM : (first + h + 1) * HDIM] for h in range(KVHEADS)], axis=0
    )


def softmax_part(scores, values):
    highest = jnp.max(scores, axis=0, keepdims=True)
    weights = jnp.exp(scores - highest)
    total = jnp.sum(weights, axis=0, keepdims=True)
    numerator = lax.dot_general(
        weights.astype(jnp.bfloat16),
        values,
        (((0,), (0,)), ((), ())),
        preferred_element_type=jnp.float32,
    )
    return highest, total, numerator


def prompt_kernel(samples, *refs):
    query_refs, cache_ref, out_refs = refs[:samples], refs[samples], refs[samples + 1 :]
    prompts, tokens, _ = cache_ref.shape
    heads = query_refs[0].shape[1]
    marks = [[] for _ in range(samples // 2)]
    for p in range(prompts):
        rows = cache_ref[p]
        keys, values = stacked_heads(rows, 0), stacked_heads(rows, KVHEADS)
        for pair in range(samples // 2):
            query = jnp.concatenate([query_refs[2 * pair][p], query_refs[2 * pair + 1][p]], axis=0)
            scores = block_scores(keys, query, tokens, heads // KVHEADS, None)
            highest, total, numerator = softmax_part(scores, values)
            out_refs[2 * pair][p] = numerator[:heads].astype(jnp.bfloat16)
            out_refs[2 * pair + 1][p] = numerator[heads:].astype(jnp.bfloat16)
            marks[pair].append((highest, total))
    for pair, found in enumerate(marks):
        highest = jnp.concatenate([m[0] for m in found], axis=0)
        total = jnp.concatenate([m[1] for m in found], axis=0)
        rows = in_parts(highest, 3) + in_parts(total, 2)
        spare = out_refs[0].shape[0] * heads - prompts * (heads + len(rows))
        rows = rows + [jnp.zeros((spare, rows[0].shape[1]), jnp.float32)]
        slab = jnp.concatenate(rows, axis=0).astype(jnp.bfloat16)
        for i in range(slab.shape[0] // heads):
            for k in (2 * pair, 2 * pair + 1):
                out_refs[k][prompts + i] = slab[i * heads : (i + 1) * heads]


def in_parts(values, count):
    parts = []
    for _ in range(count):
        parts.append(values.astype(jnp.bfloat16).astype(jnp.float32))
        values = values - parts[-1]
    return parts


def gen_kernel(length_ref, query_ref, cache_ref, out_ref, stat_ref):
    prompts, tokens, _ = cache_ref.shape
    heads = query_ref.shape[1]
    for p in range(prompts):
        rows = cache_ref[p]
        keys, values = stacked_heads(rows, 0), stacked_heads(rows, KVHEADS)
        scores = block_scores(keys, query_ref[p], tokens, heads // KVHEADS, length_ref[p])
        highest, total, numerator = softmax_part(scores, values)
        out_ref[p] = numerator
        stat_ref[0, p : p + 1, :] = highest
        stat_ref[1, p : p + 1, :] = total


VMEM_SPEC = pl.BlockSpec(memory_space=pltpu.VMEM)
ANY_SPEC = pl.BlockSpec(memory_space=pl.ANY)
SMEM_SPEC = pl.BlockSpec(memory_space=pltpu.SMEM)


def in_hbm(array):
    return pltpu.with_memory_space_constraint(array, pltpu.HBM)


def fetch_kernel(source_ref, target_ref, sems):
    pieces = sems.shape[0]
    step = source_ref.shape[0] // pieces
    copies = [
        pltpu.make_async_copy(
            source_ref.at[pl.ds(i * step, step)], target_ref.at[pl.ds(i * step, step)], sems.at[i]
        )
        for i in range(pieces)
    ]
    for copy in copies:
        copy.start()
    for copy in copies:
        copy.wait()


def fetch(array):
    return pl.pallas_call(
        fetch_kernel,
        out_shape=jax.ShapeDtypeStruct(array.shape, array.dtype),
        in_specs=[ANY_SPEC],
        out_specs=VMEM_SPEC,
        scratch_shapes=[pltpu.SemaphoreType.DMA((math.gcd(array.shape[0], 12),))],
        compiler_params=pltpu.CompilerParams(vmem_limit_bytes=MIB),
        cost_estimate=pl.CostEstimate(flops=0, bytes_accessed=4 * array.size, transcendentals=0),
    )(in_hbm(array))


def prompt_part(queries, cache):
    samples = len(queries)
    prompts, heads, _ = queries[0].shape
    slabs = -(-5 * prompts // heads)
    return pl.pallas_call(
        functools.partial(prompt_kernel, samples),
        out_shape=[jax.ShapeDtypeStruct((prompts + slabs, heads, HDIM), jnp.bfloat16)] * samples,
        in_specs=[VMEM_SPEC] * (samples + 1),
        out_specs=[VMEM_SPEC] * samples,
        compiler_params=pltpu.CompilerParams(vmem_limit_bytes=SCOPED),
        cost_estimate=pl.CostEstimate(
            flops=1000 * 1000 * 1000, bytes_accessed=4 * MIB, transcendentals=500 * 1000
        ),
    )(*queries, cache)


def part_marks(part, prompts, k):
    heads = part.shape[1]
    slab = part[prompts:].reshape(-1, HDIM)[:, k % 2 * heads : (k % 2 + 1) * heads]
    slab = slab.astype(jnp.float32)
    rows = [slab[i * prompts : (i + 1) * prompts] for i in range(5)]
    return rows[0] + rows[1] + rows[2], rows[3] + rows[4]


def gen_part(query, cache, lengths):
    shape = query.shape
    return pl.pallas_call(
        gen_kernel,
        out_shape=[
            jax.ShapeDtypeStruct(shape, jnp.float32),
            jax.ShapeDtypeStruct((2, shape[0], shape[1]), jnp.float32),
        ],
        in_specs=[SMEM_SPEC, VMEM_SPEC, VMEM_SPEC],
        out_specs=[VMEM_SPEC, VMEM_SPEC],
        compiler_params=pltpu.CompilerParams(vmem_limit_bytes=SCOPED),
        cost_estimate=pl.CostEstimate(
            flops=100 * 1000 * 1000, bytes_accessed=2 * MIB, transcendentals=100 * 1000
        ),
    )(lengths, query, cache)


def project_kernel(samples, features, place_ref, *refs):
    attended_refs = refs[:samples]
    weight_ref, residual_ref, gain_ref, mixed_ref, row_ref, order_ref = refs[samples:]
    prompts = attended_refs[0].shape[0]
    stacked = jnp.concatenate([r[...] for r in attended_refs], axis=0)
    total = jnp.dot(stacked, weight_ref[...], preferred_element_type=jnp.float32)
    for k in range(samples):
        s = lax.rem(place_ref[0] - k + samples, samples)
        order_ref[pl.ds(pl.multiple_of(s * prompts, prompts), prompts), :] = total[
            k * prompts : (k + 1) * prompts, :
        ]
    projected = order_ref[...]
    mixed_ref[...] = projected.astype(jnp.bfloat16)
    stream = residual_ref[...].astype(jnp.float32) + projected
    square = jnp.sum(stream * stream, axis=1, keepdims=True)
    high = square.astype(jnp.bfloat16).astype(jnp.float32)
    low = square - high
    row_ref[:, :features] = (stream * gain_ref[...]).astype(jnp.bfloat16)
    lane = lax.broadcasted_iota(jnp.int32, (square.shape[0], HDIM), 1)
    row_ref[:, features:] = jnp.where(lane == 0, high, jnp.where(lane == 1, low, 0.0)).astype(
        jnp.bfloat16
    )


def project(attended, out_proj, residual, gain, place):
    samples = len(attended)
    prompts, inner = attended[0].shape
    width = out_proj.shape[1]
    rows = samples * prompts
    return pl.pallas_call(
        functools.partial(project_kernel, samples, width),
        out_shape=[
            jax.ShapeDtypeStruct((rows, width), jnp.bfloat16),
            jax.ShapeDtypeStruct((rows, width + HDIM), jnp.bfloat16),
        ],
        in_specs=[SMEM_SPEC] + [VMEM_SPEC] * (samples + 3),
        out_specs=[VMEM_SPEC] * 2,
        scratch_shapes=[pltpu.VMEM((rows, width), jnp.float32)],
        compiler_params=pltpu.CompilerParams(vmem_limit_bytes=SCOPED),
        cost_estimate=pl.CostEstimate(
            flops=2 * rows * inner * width, bytes_accessed=2 * inner * width, transcendentals=0
        ),
    )(place, *attended, out_proj, residual, gain)


def gate_kernel(
    features, expert, place_ref, pick_ref, near_ref, far_ref, extra_ref, weight_ref, *refs
):
    slots = pick_ref.shape[0]
    keep_refs, give_ref, held_ref, sems = refs[:-3], refs[-3], refs[-2], refs[-1]
    half = near_ref.shape[0]
    samples = 2 * len(keep_refs)
    hidden = weight_ref.shape[2] // 2
    part = hidden // samples
    order = list(range(1, samples, 2)) + list(range(samples - 2, -1, -2))
    copies = {}
    for m in order:
        column = lax.bitwise_xor(place_ref[0], m) * part
        for side in range(2):
            columns = pl.ds(pl.multiple_of(side * hidden + column, HDIM), part)
            copies[m, side] = pltpu.make_async_copy(
                weight_ref.at[expert, :, columns], held_ref.at[m, side], sems.at[m, side]
            )
            copies[m, side].start()
    pick = pick_ref[...]
    chosen = jnp.dot(
        pick[:, :half], near_ref[:, :features], preferred_element_type=jnp.float32
    ) + jnp.dot(pick[:, half:], far_ref[:, :features], preferred_element_type=jnp.float32)
    chosen = chosen.astype(jnp.bfloat16)
    for m in order:
        out_ref = give_ref.at[m // 2] if m % 2 else keep_refs[m // 2]
        for side in range(2):
            copies[m, side].wait()
            columns = slice(side * part, (side + 1) * part)
            share = jnp.dot(chosen, held_ref[m, side], preferred_element_type=jnp.float32)
            if out_ref.shape[0] > slots:
                share = jnp.concatenate([share, extra_ref[:, columns]], axis=0)
            out_ref[:, columns] = share.astype(jnp.bfloat16)


def held_gate_kernel(features, place_ref, pick_ref, near_ref, far_ref, weight_ref, *out_refs):
    keep_refs, give_ref = out_refs[:-1], out_refs[-1]
    half = near_ref.shape[0]
    samples = 2 * len(keep_refs)
    hidden = weight_ref.shape[1] // 2
    part = hidden // samples
    pick = pick_ref[...]
    chosen = jnp.dot(
        pick[:, :half], near_ref[:, :features], preferred_element_type=jnp.float32
    ) + jnp.dot(pick[:, half:], far_ref[:, :features], preferred_element_type=jnp.float32)
    chosen = chosen.astype(jnp.bfloat16)
    for m in range(samples):
        out_ref = give_ref.at[m // 2] if m % 2 else keep_refs[m // 2]
        column = lax.bitwise_xor(place_ref[0], m) * part
        for side in range(2):
            columns = pl.ds(pl.multiple_of(side * hidden + column, HDIM), part)
            out_ref[:, side * part : (side + 1) * part] = jnp.dot(
                chosen, weight_ref[:, columns], preferred_element_type=jnp.float32
            ).astype(jnp.bfloat16)


def held_gate_up_parts(pick, near, far, weights, place, samples):
    slots = pick.shape[0]
    features, wide = weights.shape
    part = wide // 2 // samples
    one = jax.ShapeDtypeStruct((slots, 2 * part), jnp.bfloat16)
    results = pl.pallas_call(
        functools.partial(held_gate_kernel, features),
        out_shape=[one] * (samples // 2)
        + [jax.ShapeDtypeStruct((samples // 2, slots, 2 * part), jnp.bfloat16)],
        in_specs=[SMEM_SPEC] + [VMEM_SPEC] * 4,
        out_specs=[VMEM_SPEC] * (samples // 2 + 1),
        compiler_params=pltpu.CompilerParams(vmem_limit_bytes=SCOPED),
        cost_estimate=pl.CostEstimate(
            flops=2 * slots * features * wide, bytes_accessed=2 * features * wide, transcendentals=0
        ),
    )(place, pick, near, far, weights)
    return list(results[:-1]), results[-1]


def fetch_one(array, index):
    def kernel(source_ref, target_ref, sem):
        copy = pltpu.make_async_copy(source_ref.at[index], target_ref, sem)
        copy.start()
        copy.wait()

    return pl.pallas_call(
        kernel,
        out_shape=jax.ShapeDtypeStruct(array.shape[1:], array.dtype),
        in_specs=[ANY_SPEC],
        out_specs=VMEM_SPEC,
        scratch_shapes=[pltpu.SemaphoreType.DMA],
        compiler_params=pltpu.CompilerParams(vmem_limit_bytes=MIB),
        cost_estimate=pl.CostEstimate(flops=0, bytes_accessed=4 * array[0].size, transcendentals=0),
    )(in_hbm(array))


def gate_up_parts(pick, near, far, extra, weights, expert, place, samples):
    slots, rows = pick.shape
    more = extra.shape[0] if expert == CARRIER else 0
    _, features, wide = weights.shape
    hidden = wide // 2
    part = hidden // samples
    if part % HDIM:
        chosen = jnp.dot(
            pick,
            jnp.concatenate([near, far], axis=0)[:, :features],
            preferred_element_type=jnp.float32,
        ).astype(jnp.bfloat16)
        shares = jnp.dot(chosen, weights[expert], preferred_element_type=jnp.float32)
        shares = shares.astype(jnp.bfloat16).reshape(slots, 2, samples, part)
        wanted = (jnp.bitwise_xor(place[0], jnp.arange(samples))[:, None] == jnp.arange(samples)).astype(
            jnp.bfloat16
        )
        shares = jnp.einsum("mn,sgnp->msgp", wanted, shares, preferred_element_type=jnp.float32)
        shares = shares.astype(jnp.bfloat16).reshape(samples, slots, 2 * part)
        behind = jnp.broadcast_to(extra.astype(jnp.bfloat16)[:more], (samples, more, 2 * part))
        shares = jnp.concatenate([shares, behind], axis=1)
        return [shares[m] for m in range(0, samples, 2)], shares[1::2]
    one = jax.ShapeDtypeStruct((slots + more, 2 * part), jnp.bfloat16)
    results = pl.pallas_call(
        functools.partial(gate_kernel, features, expert),
        out_shape=[one] * (samples // 2)
        + [jax.ShapeDtypeStruct((samples // 2, slots + more, 2 * part), jnp.bfloat16)],
        in_specs=[SMEM_SPEC] + [VMEM_SPEC] * 4 + [ANY_SPEC],
        out_specs=[VMEM_SPEC] * (samples // 2 + 1),
        scratch_shapes=[
            pltpu.VMEM((samples, 2, features, part), jnp.bfloat16),
            pltpu.SemaphoreType.DMA((samples, 2)),
        ],
        compiler_params=pltpu.CompilerParams(vmem_limit_bytes=SCOPED + 2 * features * wide),
        cost_estimate=pl.CostEstimate(
            flops=2 * slots * features * wide, bytes_accessed=2 * features * wide, transcendentals=0
        ),
    )(place, pick, near, far, extra, in_hbm(weights))
    return results[:-1], results[-1]


def reduce_parts(keep, arrived, samples, after):
    bits = 1
    while True:
        keep = [a.astype(jnp.float32) + arrived[i].astype(jnp.float32) for i, a in enumerate(keep)]
        bits *= 2
        if bits == samples:
            return keep[0]
        give = jnp.stack([a.astype(jnp.bfloat16) for a in keep[1::2]])
        if after is not None:
            give, _ = lax.optimization_barrier((give, after))
        arrived = swap(give, "sample", samples, bits)
        keep = keep[0::2]


def gather_parts(act, samples):
    held, order, bits = [act], [0], samples // 2
    while bits > 1:
        arrived = swap(jnp.stack(held), "sample", samples, bits)
        held = held + [arrived[i] for i in range(len(held))]
        order = order + [m + bits for m in order]
        bits //= 2
    near = jnp.stack(held)
    return near, swap(near, "sample", samples, 1), order


def down_kernel(order, place_ref, *refs):
    pick_ref, weight_ref, near_out_ref, far_out_ref = refs[-4:]
    experts = weight_ref.shape[0]
    part = refs[0].shape[2]
    half = near_out_ref.shape[0]
    near_sum = far_sum = None
    for j in range(experts):
        total = None
        for n, m in enumerate(order):
            for odd in range(2):
                row = pl.multiple_of(lax.bitwise_xor(place_ref[0], m + odd) * part, HDIM)
                share = jnp.dot(
                    refs[2 * j + odd][n], weight_ref[j, pl.ds(row, part)], preferred_element_type=jnp.float32
                )
                total = share if total is None else total + share
        finished = total.astype(jnp.bfloat16)
        given = lax.dot_general(
            pick_ref[j], finished, (((0,), (0,)), ((), ())), preferred_element_type=jnp.float32
        )
        near_sum = given[:half] if near_sum is None else near_sum + given[:half]
        far_sum = given[half:] if far_sum is None else far_sum + given[half:]
    near_out_ref[...] = near_sum
    far_out_ref[...] = far_sum.astype(jnp.bfloat16)


def down_rows(acts, order, pick, weights, place):
    pairs, slots, part = acts[0].shape
    experts, hidden, width = weights.shape
    half = pick.shape[2] // 2
    shapes = [
        jax.ShapeDtypeStruct((half, width), jnp.float32),
        jax.ShapeDtypeStruct((half, width), jnp.bfloat16),
    ]
    if part % HDIM:
        known = jnp.array(order + [m + 1 for m in order], jnp.int32)
        held = jnp.bitwise_xor(place[0], known)[None, :] == jnp.arange(2 * pairs)[:, None]
        total = jnp.zeros((2 * half, width), jnp.float32)
        for j in range(experts):
            joined = jnp.einsum(
                "ni,isp->snp",
                held.astype(jnp.bfloat16),
                jnp.concatenate(acts[2 * j : 2 * j + 2], axis=0),
                preferred_element_type=jnp.float32,
            )
            joined = joined.astype(jnp.bfloat16).reshape(slots, hidden)
            finished = jnp.dot(joined, weights[j], preferred_element_type=jnp.float32)
            total = total + lax.dot_general(
                pick[j],
                finished.astype(jnp.bfloat16),
                (((0,), (0,)), ((), ())),
                preferred_element_type=jnp.float32,
            )
        return total[:half], total[half:].astype(jnp.bfloat16)
    return pl.pallas_call(
        functools.partial(down_kernel, order),
        out_shape=shapes,
        in_specs=[SMEM_SPEC] + [VMEM_SPEC] * (2 * experts + 1) + [VMEM_SPEC],
        out_specs=[VMEM_SPEC] * 2,
        compiler_params=pltpu.CompilerParams(vmem_limit_bytes=SCOPED),
        cost_estimate=pl.CostEstimate(
            flops=2 * experts * slots * hidden * width,
            bytes_accessed=2 * experts * hidden * width,
            transcendentals=0,
        ),
    )(place, *acts, pick, weights)


def gather_experts(array, owners):
    near = jnp.concatenate(
        [array] + [swap(array, "expert", owners, b) for b in range(2, owners, 2)], axis=0
    )
    return near, swap(near, "expert", owners, 1)


def on_device(
    queries,
    prompt_kv,
    gen_kv,
    gen_lengths,
    out_proj,
    residual,
    norm_gain,
    w_gate_up,
    w_down,
    routes,
    route_probs,
):
    samples, owners = lax.axis_size("sample"), lax.axis_size("expert")
    place = lax.axis_index("sample").astype(jnp.int32).reshape(1)
    prompts = queries.shape[0]
    heads = queries.shape[2] // HDIM
    width = residual.shape[2]
    rows = prompts * samples
    per_owner = w_gate_up.shape[0]
    hidden = w_down.shape[1]

    query = queries.reshape(prompts, heads, HDIM)
    all_queries = [query] + [send(query, "sample", samples, k) for k in range(1, samples)]

    gen_out, gen_stat = gen_part(query, gen_kv[:, 0], gen_lengths[:, 0])
    prompt_kv, _ = lax.optimization_barrier((prompt_kv, gen_out))
    parts = list(prompt_part(all_queries, fetch(prompt_kv)))
    parts = [parts[0]] + [send(parts[k], "sample", samples, -k) for k in range(1, samples)]
    routes, route_probs, parts[-1] = lax.optimization_barrier((routes, route_probs, parts[-1]))
    by_sample = lambda a: jnp.swapaxes(a, 0, 1).reshape(rows, TOPK)
    table = jnp.concatenate(
        [by_sample(routes).astype(jnp.float32), by_sample(route_probs)], axis=1
    )
    table = jnp.concatenate(gather_experts(table, owners), axis=0)
    capacity = 5 * rows * TOPK // (4 * per_owner * owners)
    slots = owners * capacity
    first = lax.axis_index("expert") * per_owner
    mine = (first + jnp.arange(per_owner, dtype=jnp.int32)).astype(jnp.float32)
    match = table[None, :, :TOPK] == mine[:, None, None]
    hit = jnp.any(match, axis=2)
    weight = jnp.sum(jnp.where(match, table[None, :, TOPK:], 0.0), axis=2)
    hit_blocks = hit.reshape(per_owner, owners, rows)
    earlier = (jnp.arange(rows)[:, None] < jnp.arange(rows)[None, :]).astype(jnp.bfloat16)
    rank = jnp.einsum(
        "jbr,rq->jbq",
        hit_blocks.astype(jnp.bfloat16),
        earlier,
        preferred_element_type=jnp.float32,
    ).astype(jnp.int32)
    slot = rank + capacity * jnp.arange(owners, dtype=jnp.int32)[None, :, None]
    slot = jnp.where(hit_blocks, slot, -1).reshape(per_owner, owners * rows)
    chosen = slot[:, None, :] == jnp.arange(slots, dtype=jnp.int32)[None, :, None]
    pick = chosen.astype(jnp.bfloat16)
    slot_weight = jnp.sum(jnp.where(chosen, weight[:, None, :], 0.0), axis=2)

    outs = [gen_out] + [part[:prompts] for part in parts]
    marks = [(gen_stat[0], gen_stat[1])] + [
        part_marks(part, prompts, k) for k, part in enumerate(parts)
    ]
    highest = functools.reduce(jnp.maximum, [m[0] for m in marks])
    scales = [jnp.exp(m[0] - highest) for m in marks]
    total = sum(c * m[1] for c, m in zip(scales, marks))
    attended = sum(
        o.astype(jnp.float32) * (c / total)[:, :, None] for o, c in zip(outs, scales)
    )
    attended = attended.astype(jnp.bfloat16).reshape(prompts, heads * HDIM)
    out_proj, _, pick, chosen, slot_weight = lax.optimization_barrier(
        (out_proj, attended, pick, chosen, slot_weight)
    )
    out_proj = fetch(out_proj)
    attended = [attended] + [send(attended, "sample", samples, k) for k in range(1, samples)]
    mixed, row_block = project(
        attended,
        out_proj,
        jnp.swapaxes(residual, 0, 1).reshape(rows, width),
        norm_gain.reshape(1, width),
        place,
    )
    mixed = jnp.swapaxes(mixed.reshape(samples, prompts, width), 0, 1)

    near, far = gather_experts(row_block, owners)
    part = hidden // samples
    square = jnp.concatenate([near[:, width : width + 2], far[:, width : width + 2]], axis=0)
    square = square.astype(jnp.float32).T.reshape(-1)
    total_rows = owners * rows
    extra_rows = -(-2 * total_rows // (16 * part)) * 8
    extra = jnp.pad(square, (0, extra_rows * 2 * part - square.size)).reshape(extra_rows, 2 * part)
    sums = {}
    for j in reversed(range(per_owner)):
        if j == 1 and part % HDIM == 0:
            source, _ = lax.optimization_barrier((w_gate_up, row_block))
            held = fetch_one(source, j)
            keep, give = held_gate_up_parts(pick[j], near, far, held, place, samples)
        else:
            keep, give = gate_up_parts(pick[j], near, far, extra, w_gate_up, j, place, samples)
        arrived = swap(give, "sample", samples, 1)
        sums[j] = keep, arrived
    acts = [None] * (2 * per_owner)
    for j in [CARRIER] + [j for j in range(per_owner) if j != CARRIER]:
        gate_up = reduce_parts(*sums[j], samples, first_act if j == 1 else None)
        if j == CARRIER:
            square = gate_up[slots:].reshape(-1)
            square = square[:total_rows] + square[total_rows : 2 * total_rows]
            factor = lax.rsqrt(square / (width * samples) + EPSILON)
            slot_factor = jnp.sum(jnp.where(chosen, factor[None, None, :], 0.0), axis=2)
            gate_up = gate_up[:slots]
        gate_up = gate_up * slot_factor[j][:, None]
        act = jax.nn.silu(gate_up[:, :part]) * gate_up[:, part:] * slot_weight[j][:, None]
        act = act.astype(jnp.bfloat16)
        first_act = act if j == 0 else first_act
        act_near, act_far, order = gather_parts(act, samples)
        acts[2 * j : 2 * j + 2] = act_near, act_far
    w_down, acts[-2] = lax.optimization_barrier((w_down, acts[-2]))
    w_down = fetch(w_down)
    kept, given = down_rows(acts, order, pick, w_down, place)
    kept = kept.reshape(owners // 2, rows, width)
    arrived = swap(given.reshape(owners // 2, rows, width), "expert", owners, 1)
    paired = kept + arrived.astype(jnp.float32)
    outgoing = paired.astype(jnp.bfloat16)
    combined = paired[0]
    for b in range(1, owners // 2):
        combined = combined + swap(outgoing[b], "expert", owners, 2 * b).astype(jnp.float32)
    expert_out = combined.astype(jnp.bfloat16).reshape(samples, prompts, width)
    return mixed, jnp.swapaxes(expert_out, 0, 1)


def solution(mesh):
    placed = (
        P("expert", "sample", None),
        P("expert", "sample", None),
        P("expert", "sample", None, None),
        P("expert", "sample"),
        P(None, "sample"),
        P("expert", None, "sample"),
        P("sample"),
        P("expert", "sample", None),
        P("expert", None, "sample"),
        P("expert", None, None),
        P("expert", None, None),
    )
    return jax.shard_map(
        on_device,
        mesh=mesh,
        in_specs=placed,
        out_specs=(P("expert", None, "sample"), P("expert", None, "sample")),
        check_vma=False,
    )
```
